256 devices in a mesh: replica: 32 (over z_hi, x, core), fsdp: 8 (over z_lo, y).
Axes of the slice: x: 4, y: 4, z: 8 (z_hi: 4, z_lo: 2; z = z_hi * 2 + z_lo), core: 2. Of those that a mesh axis runs over, the one named last changes fastest.
Arguments:
- layer_input: bfloat16 [32, 2, 1024, 12288], P('replica', None, 'fsdp'), may hold values from -6 to 6
- cotangent: bfloat16 [32, 2, 1024, 256], P('replica', None, 'fsdp'), may hold values from -6 to 6
- weight: bfloat16 [32, 12288, 256], P('replica', 'fsdp'), may hold values from -5 to 5
- first_moment: float32 [32, 12288, 256], P('replica', 'fsdp'), may hold values from -0.2 to 0.2
- second_moment: float32 [32, 12288, 256], P('replica', 'fsdp'), may hold values from 0.01 to 0.1
- key_gain: float32 [128], replicated, may hold values from 0.5 to 1.5
- frag_index: int32 [1], replicated, may hold values from 0 to 4095
- anchor: float32 [12288, 128], P('fsdp'), may hold values from -5 to 5
- momentum: float32 [12288, 128], P('fsdp'), may hold values from -3 to 3
Outputs:
- merged_weight: bfloat16 [32, 12288, 256], P('replica', 'fsdp')
- new_momentum: float32 [12288, 128], P('fsdp')
- new_anchor: float32 [12288, 128], P('fsdp')
The draws below stay inside these ranges and needn't reach their ends.
Inputs may be any that keep to these rules, and one draw needn't show every extreme that they name: `frag_index`: the same plan position for all replicas.
All inputs are finite; a program needn't handle non-finite values.
Results may differ from the reference program's by a relative error of at most 0.014.
Values may be sent and summed in bfloat16 or wider, within the bound.
A program may use at most 128 MiB of HBM per device.

```python
import math
import jax
import jax.numpy as jnp
from jax import lax

D = 12288
HEAD = 128
KV = 2
C = 256
TOK_DEV = 128
STEPS = 2
RTOK = 1024
REPLICAS = 32
N_REPLICA = 32
N_FSDP = 8


def block_scale(own_key, extent, pieces, low, top_value):
    def one(position, parts):
        steps = jax.random.uniform(jax.random.fold_in(jax.random.fold_in(own_key, 6), position), (parts,), jnp.float32, low / len(pieces), top_value / len(pieces))
        return jnp.repeat(jnp.exp(steps), extent[position] // parts).reshape((-1,) + (1,) * (len(extent) - position - 1))

    loudness = one(*pieces[0])
    for cut in pieces[1:]:
        loudness = loudness * one(*cut)
    return loudness


def gaussian(rng, extent, deviation, reach, pieces=(), dtype=jnp.bfloat16):
    values = deviation * jax.random.normal(rng, extent, jnp.float32)
    if pieces:
        values = values * block_scale(rng, extent, pieces, -0.22, 0.18)
    return jnp.clip(values, -reach, reach).astype(dtype)


def setup_inputs(seed: int = 0) -> dict:
    keys = jax.random.split(jax.random.key(seed), 10)
    return {
        "layer_input": gaussian(keys[0], (REPLICAS, STEPS, RTOK, D), 1.0, 6.0, ((0, 32), (2, 8))),
        "cotangent": gaussian(keys[1], (REPLICAS, STEPS, RTOK, C), 1.0, 6.0, ((0, 32), (2, 8))),
        "weight": gaussian(keys[2], (REPLICAS, D, C), 1.0, 5.0, ((0, 32), (1, 8))),
        "first_moment": gaussian(keys[3], (REPLICAS, D, C), 0.03, 0.2, ((0, 32), (1, 8)), jnp.float32),
        "second_moment": jnp.clip(jnp.exp(math.log(0.1) - 2.3025851 * jax.random.uniform(keys[4], (REPLICAS, D, C), jnp.float32) ** block_scale(keys[4], (REPLICAS, D, C), ((0, 32), (1, 8)), -0.2, 0.2)), 0.01, 0.1),
        "key_gain": jnp.clip(1.0 + 0.1 * jax.random.normal(keys[5], (HEAD,), jnp.float32), 0.5, 1.5),
        "frag_index": jax.random.randint(keys[6], (1,), 0, 4096).astype(jnp.int32),
        "anchor": gaussian(keys[7], (D, HEAD), 1.0, 5.0, ((0, 8),), jnp.float32),
        "momentum": gaussian(keys[8], (D, HEAD), 0.5, 3.0, ((0, 8),), jnp.float32),
    }


beta_first = 0.9
beta_second = 0.95
inner_rate = 2.0
decay_rate = 0.05
adam_eps = 1e-08
norm_eps = 1e-06
outer_rate = 0.7
outer_beta = 0.9
mix_local = 0.5

def norm_backward(keys_raw, upstream, key_gain):
    tokens_count, columns = keys_raw.shape
    grouped = keys_raw.reshape(tokens_count, columns // HEAD, HEAD)
    scaled_up = upstream.astype(jnp.float32).reshape(tokens_count, columns // HEAD, HEAD) * key_gain
    inverse = lax.rsqrt(lax.optimization_barrier(jnp.mean(grouped * grouped, axis=-1, keepdims=True)) + norm_eps)
    inner_prod = lax.optimization_barrier(jnp.mean(scaled_up * grouped, axis=-1, keepdims=True))
    result = inverse * scaled_up - grouped * (inverse * inverse * inverse) * inner_prod
    return result.reshape(tokens_count, columns).astype(jnp.bfloat16)

def adamw(weight_now, moment_one, moment_two, gradient):
    moment_one = beta_first * moment_one + (1.0 - beta_first) * gradient
    moment_two = beta_second * moment_two + (1.0 - beta_second) * gradient * gradient
    master = weight_now.astype(jnp.float32)
    master = master - inner_rate * (moment_one / (jnp.sqrt(moment_two) + adam_eps) + decay_rate * master)
    return (master.astype(jnp.bfloat16), moment_one, moment_two)

def reference(layer_input, cotangent, weight, first_moment, second_moment, key_gain, frag_index, anchor, momentum):
    first_col = frag_index[0].astype(jnp.int32) % KV * HEAD
    fragment = lax.dynamic_slice_in_dim(weight, first_col, HEAD, 2).astype(jnp.float32)
    delta_mean = lax.optimization_barrier(jnp.sum(anchor[None] - fragment, axis=0)) / N_REPLICA
    new_momentum = outer_beta * momentum + delta_mean
    new_anchor = anchor - outer_rate * (delta_mean + outer_beta * new_momentum)

    def inner_run(packed):
        tokens_rep, upstream_rep, weight_now, moment_one, moment_two = packed
        for inner_step in range(STEPS):
            tokens_now = tokens_rep[inner_step]
            keys_raw = jnp.dot(tokens_now, weight_now, preferred_element_type=jnp.float32) * (1.0 / math.sqrt(D))
            delta_keys = norm_backward(keys_raw, upstream_rep[inner_step], key_gain)
            blocks = tokens_now.reshape(N_FSDP, TOK_DEV, D).astype(jnp.float32)
            delta_blocks = delta_keys.reshape(N_FSDP, TOK_DEV, KV * HEAD).astype(jnp.float32)
            block_terms = jnp.einsum('ntd,ntc->ndc', blocks, delta_blocks)
            rounded = lax.optimization_barrier(block_terms.astype(jnp.bfloat16))
            gradient = lax.optimization_barrier(jnp.sum(rounded.astype(jnp.float32), axis=0)) * (1.0 / math.sqrt(TOK_DEV * N_FSDP))
            weight_now, moment_one, moment_two = adamw(weight_now, moment_one, moment_two, gradient)
        return weight_now
    trained = lax.map(inner_run, (layer_input, cotangent, weight, first_moment, second_moment))
    local_frag = lax.dynamic_slice_in_dim(trained, first_col, HEAD, 2).astype(jnp.float32)
    mixed_cols = (mix_local * local_frag + (1.0 - mix_local) * new_anchor[None]).astype(jnp.bfloat16)
    merged_weight = lax.dynamic_update_slice_in_dim(trained, mixed_cols, first_col, 2)
    return (merged_weight, new_momentum, new_anchor)
```

```python
import math

import jax
import jax.numpy as jnp
from jax import lax
from jax.experimental import pallas as pl
from jax.experimental.pallas import tpu as pltpu
from jax.sharding import PartitionSpec as P

D = 12288
HEAD = 128
KV = 2
C = KV * HEAD
TOK = 128
STEPS = 2
FSDP = 8
ROWS = D // FSDP
REPLICAS = 32
SPLITS = (2, 4)
TILE = 256

beta_first = 0.9
beta_second = 0.95
inner_rate = 2.0
decay_rate = 0.05
adam_eps = 1e-08
norm_eps = 1e-06
outer_rate = 0.7
outer_beta = 0.9
mix_local = 0.5

PLANE = ((1, 2), (0, 2), (1, 1), (1, 3), (0, 1), (0, 3), (1, 0))
LAYER = tuple((dx, dc) for dx in (2, 1, 3, 0) for dc in (0, 1) if (dx, dc) != (0, 0))
LAYERS = (2, 1, 3)
SEG = ROWS // 8
PIECE = SEG // 4
MESH = pl.DeviceIdType.MESH


def kernel(
    x_hbm, cot_hbm, w_hbm, m_hbm, v_hbm, gain_ref, frag_ref, anchor_hbm, mom_hbm,
    merged_hbm, newmom_hbm, newanchor_hbm,
    xbuf0, xbuf1, rsend0, rsend1, rrecv0, rrecv1, dbuf0, dbuf1,
    cot, w_now, m_now, v_now, grad, anchor, mom, out_w,
    frag, layer_in, partial, pieces, total,
    loc_sem, xs0, xr0, xs1, xr1, rs, rr, ds, dr, ls, lr, ps, pr, qs, qr, ts, tr, own_sem,
):
    rep = lax.axis_index("replica")
    fs = lax.axis_index("fsdp")
    zl, yy = fs // 4, lax.rem(fs, 4)
    zh, xx, cc = rep // 8, lax.rem(rep // 2, 4), lax.rem(rep, 2)

    def plane_index(dz, dy):
        return lax.rem(zl + dz, 2) * 4 + lax.rem(yy + dy, 4)

    def layer_index(dx, dc):
        return lax.rem(xx + dx, 4) * 2 + lax.rem(cc + dc, 2)

    def plane_dev(dz, dy):
        return (rep, plane_index(dz, dy))

    def layer_dev(dx, dc):
        return (zh * 8 + layer_index(dx, dc), fs)

    def stack_dev(dh):
        return (lax.rem(zh + dh, 4) * 8 + xx * 2 + cc, fs)

    partners = (
        [plane_dev(*o) for o in PLANE] + [layer_dev(*o) for o in LAYER] + [stack_dev(h) for h in LAYERS]
    )
    with jax.named_scope("entry"):
        bar = pltpu.get_barrier_semaphore()
        for p in partners:
            pl.semaphore_signal(bar, inc=1, device_id=p, device_id_type=MESH)
        pl.semaphore_wait(bar, len(partners))

    sends = []

    def remote(src, dst, s, r, dev):
        cp = pltpu.make_async_remote_copy(
            src_ref=src, dst_ref=dst, send_sem=s, recv_sem=r, device_id=dev, device_id_type=MESH
        )
        cp.start()
        sends.append(cp)
        return cp

    def slot(dz, dy):
        return dz * 4 + dy

    def back(dz, dy):
        return dz * 4 + (4 - dy) % 4

    xbufs, xss, xrs = (xbuf0, xbuf1), (xs0, xs1), (xr0, xr1)
    rsends, rrecvs, dbufs = (rsend0, rsend1), (rrecv0, rrecv1), (dbuf0, dbuf1)
    first_unit = (0, SPLITS[0])

    def columns(dz, dy):
        return pl.ds(pl.multiple_of(plane_index(dz, dy) * ROWS, 128), ROWS)

    def send_x(step, h):
        n = TOK // SPLITS[step]
        got = []
        for i, o in enumerate(PLANE):
            got.append(
                remote(
                    x_hbm.at[0, step, pl.ds(h * n, n), columns(*o)],
                    xbufs[step].at[h, pl.ds(back(*o) * n, n)],
                    xss[step].at[h, i],
                    xrs[step].at[h, i],
                    plane_dev(*o),
                )
            )
        own = pltpu.make_async_copy(
            x_hbm.at[0, step, pl.ds(h * n, n), columns(0, 0)],
            xbufs[step].at[h, pl.ds(0, n)],
            own_sem.at[first_unit[step] + h],
        )
        own.start()
        return got, own

    def local(src, dst, i):
        cp = pltpu.make_async_copy(src, dst, loc_sem.at[i])
        cp.start()
        return cp

    xcp = {}
    with jax.named_scope("send_x"):
        for h in range(SPLITS[0]):
            xcp[0, h] = send_x(0, h)
        get_w = local(w_hbm.at[0], w_now, 0)
        get_cot = local(cot_hbm.at[0], cot, 1)
        get_m = local(m_hbm.at[0], m_now, 2)
        get_v = local(v_hbm.at[0], v_now, 3)
        get_anchor = local(anchor_hbm, anchor, 4)
        get_mom = local(mom_hbm, mom, 5)
        for h in range(SPLITS[1]):
            xcp[1, h] = send_x(1, h)

    first_frag = lax.rem(frag_ref[0], KV) == 0
    lane_first = jnp.where(first_frag, jnp.float32(1.0), jnp.float32(0.0))

    def segment(dx, dc):
        return pl.ds(pl.multiple_of(layer_index(dx, dc) * SEG, 16), SEG)

    with jax.named_scope("fragment"):
        get_w.wait()
        frag[...] = jnp.where(
            lane_first > 0.5, w_now[:, :HEAD].astype(jnp.float32), w_now[:, HEAD:].astype(jnp.float32)
        ).astype(jnp.bfloat16)
        layer_cps = []
        for i, (dx, dc) in enumerate(LAYER):
            layer_cps.append(
                remote(frag.at[segment(dx, dc)], layer_in.at[i], ls.at[i], lr.at[i], layer_dev(dx, dc))
            )

    width_scale = 1.0 / math.sqrt(D)
    token_scale = 1.0 / math.sqrt(TOK * FSDP)
    unit = lambda step, h: first_unit[step] + h
    rcp, dcp = {}, {}

    def stage_raw(step, h):
        n = TOK // SPLITS[step]
        got, own = xcp[step, h]
        with jax.named_scope(f"wait_x_{step}_{h}"):
            own.wait()
            for cp in got:
                cp.wait_recv()
        with jax.named_scope(f"raw_{step}_{h}"):
            rsends[step][h] = jnp.dot(
                xbufs[step][h], w_now[...], preferred_element_type=jnp.float32
            ).astype(jnp.bfloat16)
            cps = []
            for i, o in enumerate(PLANE):
                cps.append(
                    remote(
                        rsends[step].at[h, pl.ds(slot(*o) * n, n)],
                        rrecvs[step].at[h, i],
                        rs.at[unit(step, h), i],
                        rr.at[unit(step, h), i],
                        plane_dev(*o),
                    )
                )
            rcp[step, h] = cps

    def stage_delta(step, h):
        n = TOK // SPLITS[step]
        with jax.named_scope(f"wait_raw_{step}_{h}"):
            for cp in rcp[step, h]:
                cp.wait_recv()
        with jax.named_scope(f"delta_{step}_{h}"):
            raw = rsends[step][h, :n].astype(jnp.float32)
            for i in range(len(PLANE)):
                raw = raw + rrecvs[step][h, i].astype(jnp.float32)
            raw = raw * width_scale
            up = cot[step, pl.ds(h * n, n)].astype(jnp.float32)
            gain = gain_ref[...]
            for k in range(KV):
                cols = slice(k * HEAD, (k + 1) * HEAD)
                g = raw[:, cols]
                p = up[:, cols] * gain
                inv = lax.rsqrt(jnp.mean(g * g, axis=-1, keepdims=True) + norm_eps)
                dotp = jnp.mean(p * g, axis=-1, keepdims=True)
                dbufs[step][h, :n, cols] = (inv * p - g * (inv * inv * inv) * dotp).astype(jnp.bfloat16)
            cps = []
            for i, o in enumerate(PLANE):
                cps.append(
                    remote(
                        dbufs[step].at[h, pl.ds(0, n)],
                        dbufs[step].at[h, pl.ds(back(*o) * n, n)],
                        ds.at[unit(step, h), i],
                        dr.at[unit(step, h), i],
                        plane_dev(*o),
                    )
                )
            dcp[step, h] = cps

    def stage_grad(step, h, finish):
        with jax.named_scope(f"wait_delta_{step}_{h}"):
            for cp in dcp[step, h]:
                cp.wait_recv()
        with jax.named_scope(f"grad_{step}_{h}"):
            d = dbufs[step][h]
            for t in range(ROWS // TILE):
                rows = pl.ds(t * TILE, TILE)
                g = lax.dot_general(
                    xbufs[step][h, :, rows], d, (((0,), (0,)), ((), ())), preferred_element_type=jnp.float32
                )
                if h > 0:
                    g = g + grad[rows]
                if finish is None:
                    grad[rows] = g
                else:
                    finish(rows, g * token_scale)

    def adamw(rows, g):
        m = beta_first * m_now[rows] + (1.0 - beta_first) * g
        v = beta_second * v_now[rows] + (1.0 - beta_second) * g * g
        w = w_now[rows].astype(jnp.float32)
        w = w - inner_rate * (m / (jnp.sqrt(v) + adam_eps) + decay_rate * w)
        return w.astype(jnp.bfloat16), m, v

    def finish_first(rows, g):
        w, m, v = adamw(rows, g)
        w_now[rows] = w
        m_now[rows] = m
        v_now[rows] = v

    def finish_last(rows, g):
        w, _, _ = adamw(rows, g)
        mixed = anchor[rows]
        for k in range(KV):
            cols = slice(k * HEAD, (k + 1) * HEAD)
            mine = w[:, cols].astype(jnp.float32)
            chosen = lane_first > 0.5 if k == 0 else lane_first < 0.5
            out_w[rows, cols] = jnp.where(
                chosen, mix_local * mine + (1.0 - mix_local) * mixed, mine
            ).astype(jnp.bfloat16)

    def layer_sum():
        with jax.named_scope("layer_sum"):
            for cp in layer_cps:
                cp.wait_recv()
            s = frag[segment(0, 0)].astype(jnp.float32)
            for i in range(len(LAYER)):
                s = s + layer_in[i].astype(jnp.float32)
            partial[...] = s
            cps = []
            for i, dh in enumerate(LAYERS):
                where = pl.ds(pl.multiple_of(lax.rem(zh + dh, 4) * PIECE, 8), PIECE)
                cps.append(remote(partial.at[where], pieces.at[i], ps.at[i], pr.at[i], stack_dev(dh)))
            return cps

    def stack_sum(cps):
        with jax.named_scope("stack_sum"):
            for cp in cps:
                cp.wait_recv()
            s = partial[pl.ds(pl.multiple_of(zh * PIECE, 8), PIECE)]
            for i in range(len(LAYERS)):
                s = s + pieces[i]
            mine = pl.ds(pl.multiple_of(layer_index(0, 0) * SEG + zh * PIECE, 8), PIECE)
            total[mine] = s
            out = []
            for i, dh in enumerate(LAYERS):
                out.append(remote(total.at[mine], total.at[mine], qs.at[i], qr.at[i], stack_dev(dh)))
            return out

    def layer_gather(cps):
        with jax.named_scope("layer_gather"):
            for cp in cps:
                cp.wait_recv()
            out = []
            for i, (dx, dc) in enumerate(LAYER):
                out.append(
                    remote(
                        total.at[segment(0, 0)], total.at[segment(0, 0)], ts.at[i], tr.at[i], layer_dev(dx, dc)
                    )
                )
            return out

    def outer(cps):
        with jax.named_scope("outer"):
            for cp in cps:
                cp.wait_recv()
            get_anchor.wait()
            get_mom.wait()
            a = anchor[...]
            mean = a - total[...] * (1.0 / REPLICAS)
            nm = outer_beta * mom[...] + mean
            mom[...] = nm
            anchor[...] = a - outer_rate * (mean + outer_beta * nm)
            return [local(mom, newmom_hbm, 4), local(anchor, newanchor_hbm, 5)]

    stage_raw(0, 0)
    get_cot.wait()
    stage_delta(0, 0)
    layer_out = layer_sum()
    stage_raw(0, 1)
    stage_delta(0, 1)
    get_m.wait()
    get_v.wait()
    stage_grad(0, 0, None)
    stack_out = stack_sum(layer_out)
    stage_grad(0, 1, finish_first)
    gather_out = layer_gather(stack_out)
    last = SPLITS[1] - 1
    stage_raw(1, 0)
    stage_delta(1, 0)
    outs = outer(gather_out)
    for h in range(1, last + 1):
        stage_raw(1, h)
        stage_grad(1, h - 1, None)
        stage_delta(1, h)
    stage_grad(1, last, finish_last)
    with jax.named_scope("write"):
        put = local(out_w, merged_hbm.at[0], 0)
        for cp in sends:
            cp.wait_send()
        for cp in outs:
            cp.wait()
        put.wait()


def body(layer_input, cotangent, weight, first_moment, second_moment, key_gain, frag_index, anchor, momentum):
    bf, f32 = jnp.bfloat16, jnp.float32
    units = sum(SPLITS)
    dma = pltpu.SemaphoreType.DMA
    any_spec = pl.BlockSpec(memory_space=pl.ANY)
    scratch = [
        pltpu.VMEM((SPLITS[0], TOK * FSDP // SPLITS[0], ROWS), bf),
        pltpu.VMEM((SPLITS[1], TOK * FSDP // SPLITS[1], ROWS), bf),
        pltpu.VMEM((SPLITS[0], TOK * FSDP // SPLITS[0], C), bf),
        pltpu.VMEM((SPLITS[1], TOK * FSDP // SPLITS[1], C), bf),
        pltpu.VMEM((SPLITS[0], 7, TOK // SPLITS[0], C), bf),
        pltpu.VMEM((SPLITS[1], 7, TOK // SPLITS[1], C), bf),
        pltpu.VMEM((SPLITS[0], TOK * FSDP // SPLITS[0], C), bf),
        pltpu.VMEM((SPLITS[1], TOK * FSDP // SPLITS[1], C), bf),
        pltpu.VMEM((STEPS, TOK, C), bf),
        pltpu.VMEM((ROWS, C), bf),
        pltpu.VMEM((ROWS, C), f32),
        pltpu.VMEM((ROWS, C), f32),
        pltpu.VMEM((ROWS, C), f32),
        pltpu.VMEM((ROWS, HEAD), f32),
        pltpu.VMEM((ROWS, HEAD), f32),
        pltpu.VMEM((ROWS, C), bf),
        pltpu.VMEM((ROWS, HEAD), bf),
        pltpu.VMEM((len(LAYER), SEG, HEAD), bf),
        pltpu.VMEM((SEG, HEAD), f32),
        pltpu.VMEM((len(LAYERS), PIECE, HEAD), f32),
        pltpu.VMEM((ROWS, HEAD), f32),
        dma((6,)),
        dma((SPLITS[0], 7)),
        dma((SPLITS[0], 7)),
        dma((SPLITS[1], 7)),
        dma((SPLITS[1], 7)),
        dma((units, 7)),
        dma((units, 7)),
        dma((units, 7)),
        dma((units, 7)),
        dma((7,)),
        dma((7,)),
        dma((3,)),
        dma((3,)),
        dma((3,)),
        dma((3,)),
        dma((7,)),
        dma((7,)),
        dma((units,)),
    ]
    return pl.pallas_call(
        kernel,
        name="inner_outer",
        out_shape=(
            jax.ShapeDtypeStruct((1, ROWS, C), bf),
            jax.ShapeDtypeStruct((ROWS, HEAD), f32),
            jax.ShapeDtypeStruct((ROWS, HEAD), f32),
        ),
        in_specs=[any_spec] * 5
        + [pl.BlockSpec(memory_space=pltpu.VMEM), pl.BlockSpec(memory_space=pltpu.SMEM)]
        + [any_spec] * 2,
        out_specs=(any_spec, any_spec, any_spec),
        scratch_shapes=scratch,
        compiler_params=pltpu.CompilerParams(
            collective_id=0, has_side_effects=True, vmem_limit_bytes=62 << 20
        ),
    )(
        layer_input, cotangent, weight, first_moment, second_moment,
        key_gain.reshape(1, HEAD), frag_index, anchor, momentum,
    )


def solution(mesh):
    placed = (
        P("replica", None, "fsdp", None),
        P("replica", None, "fsdp", None),
        P("replica", "fsdp", None),
        P("replica", "fsdp", None),
        P("replica", "fsdp", None),
        P(),
        P(),
        P("fsdp", None),
        P("fsdp", None),
    )
    return jax.shard_map(
        body,
        mesh=mesh,
        in_specs=placed,
        out_specs=(P("replica", "fsdp", None), P("fsdp", None), P("fsdp", None)),
        check_vma=False,
    )
```

```python
import math

import jax
import jax.numpy as jnp
from jax import lax
from jax.experimental import pallas as pl
from jax.experimental.pallas import tpu as pltpu
from jax.sharding import PartitionSpec as P

D = 12288
HEAD = 128
KV = 2
C = KV * HEAD
TOK = 128
STEPS = 2
FSDP = 8
ROWS = D // FSDP
REPLICAS = 32
GROUPS = ((64, 64), (64, 48, 16))
SIZES = ((32, 32, 32, 32), (32, 32, 32, 16, 16))
AHEAD = 64
UNITS = tuple((s, sum(SIZES[s][:i]), n) for s in range(STEPS) for i, n in enumerate(SIZES[s]))
EXCH = tuple((s, g) for s in range(STEPS) for g in range(len(GROUPS[s])))
TILE = 256
PARTS = 2
LIMIT = 61 << 20

beta_first = 0.9
beta_second = 0.95
inner_rate = 2.0
decay_rate = 0.05
adam_eps = 1e-08
norm_eps = 1e-06
outer_rate = 0.7
outer_beta = 0.9
mix_local = 0.5

PLANE = ((1, 2), (0, 2), (1, 1), (1, 3), (0, 1), (0, 3), (1, 0))
LAYER = tuple((dx, dc) for dx in (2, 1, 3, 0) for dc in (0, 1) if (dx, dc) != (0, 0))
LAYERS = (2, 1, 3)
SEG = ROWS // 8
PIECE = SEG // 4
MESH = pl.DeviceIdType.MESH


def kernel(
    x_hbm, cot_hbm, w_hbm, m_hbm, v_hbm, gain_ref, frag_ref, anchor_hbm, mom_hbm,
    out_w, newmom, newanchor,
    *scratch,
):
    count = len(EXCH)
    xbufs = dict(zip(EXCH, scratch[:count]))
    rsends = dict(zip(EXCH, scratch[count : 2 * count]))
    rrecvs = dict(zip(EXCH, scratch[2 * count : 3 * count]))
    dbufs = dict(zip(EXCH, scratch[3 * count : 4 * count]))
    (
        cot, w_now, m_now, v_now, grad, anchor, mom, frag, layer_in, partial, pieces, total,
        loc_sem, own_sem, xs, xr, rs, rr, ds, dr, ls, lr, ps, pr, qs, qr, ts, tr, go_sem,
    ) = scratch[4 * count :]
    rep = lax.axis_index("replica")
    fs = lax.axis_index("fsdp")
    zl, yy = fs // 4, lax.rem(fs, 4)
    zh, xx, cc = rep // 8, lax.rem(rep // 2, 4), lax.rem(rep, 2)

    def plane_index(dz, dy):
        return lax.rem(zl + dz, 2) * 4 + lax.rem(yy + dy, 4)

    def layer_index(dx, dc):
        return lax.rem(xx + dx, 4) * 2 + lax.rem(cc + dc, 2)

    def plane_dev(dz, dy):
        return (rep, plane_index(dz, dy))

    def layer_dev(dx, dc):
        return (zh * 8 + layer_index(dx, dc), fs)

    def stack_dev(dh):
        return (lax.rem(zh + dh, 4) * 8 + xx * 2 + cc, fs)

    leader = rep == REPLICAS - 1
    with jax.named_scope("entry"):
        bar = pltpu.get_barrier_semaphore()
        for o in PLANE:
            pl.semaphore_signal(bar, inc=1, device_id=plane_dev(*o), device_id_type=MESH)

        @pl.when(jnp.logical_not(leader))
        def _():
            pl.semaphore_signal(bar, inc=1, device_id=(REPLICAS - 1, fs), device_id_type=MESH)
            pl.semaphore_wait(bar, len(PLANE))

        @pl.when(leader)
        def _():
            pl.semaphore_wait(bar, len(PLANE) + REPLICAS - 1)

    sends = []

    def remote(src, dst, s, r, dev):
        cp = pltpu.make_async_remote_copy(
            src_ref=src, dst_ref=dst, send_sem=s, recv_sem=r, device_id=dev, device_id_type=MESH
        )
        cp.start()
        sends.append(cp)
        return cp

    def arrive(cps, name):
        for cp in cps:
            cp.wait_recv()

    def slot(dz, dy):
        return dz * 4 + dy

    def back(dz, dy):
        return dz * 4 + (4 - dy) % 4

    def columns(dz, dy):
        return pl.ds(pl.multiple_of(plane_index(dz, dy) * ROWS, 128), ROWS)

    def place(step, row):
        g = 0
        while row >= GROUPS[step][g]:
            row -= GROUPS[step][g]
            g += 1
        return g, row

    def send_x(k):
        step, row, rows = UNITS[k]
        g, at = place(step, row)
        n = GROUPS[step][g]
        got = []
        for i, o in enumerate(PLANE):
            got.append(
                remote(
                    x_hbm.at[0, step, pl.ds(row, rows), columns(*o)],
                    xbufs[step, g].at[pl.ds(back(*o) * n + at, rows)],
                    xs.at[k, i],
                    xr.at[k, i],
                    plane_dev(*o),
                )
            )
        own = pltpu.make_async_copy(
            x_hbm.at[0, step, pl.ds(row, rows), columns(0, 0)],
            xbufs[step, g].at[pl.ds(at, rows)],
            own_sem.at[k],
        )
        own.start()
        return got, own

    def local(src, dst, i):
        cp = pltpu.make_async_copy(src, dst, loc_sem.at[i])
        cp.start()
        return cp

    xcp = {}

    def issue(k):
        if k < len(UNITS):
            with jax.named_scope("send_x"):
                xcp[k] = send_x(k)

    def landed(k):
        with jax.named_scope("wait_x"):
            got, own = xcp[k]
            own.wait()
            arrive(got, f"x_{k}")

    issued = 0
    done = 0
    position = 0

    def top_up():
        nonlocal issued, done
        while issued < len(UNITS) and (issued == 0 or sum(u[2] for u in UNITS[:issued]) < position + AHEAD):
            issue(issued)
            issued += 1

    top_up()
    get_w = local(w_hbm.at[0], w_now, 0)
    get_cot = local(cot_hbm.at[0], cot, 1)
    get_m = local(m_hbm.at[0], m_now, 2)
    get_v = local(v_hbm.at[0], v_now, 3)
    get_anchor = local(anchor_hbm, anchor, 4)
    get_mom = local(mom_hbm, mom, 5)

    first_frag = lax.rem(frag_ref[0], KV) == 0
    lane_first = jnp.where(first_frag, jnp.float32(1.0), jnp.float32(0.0))

    def segment(dx, dc):
        return pl.ds(pl.multiple_of(layer_index(dx, dc) * SEG, 16), SEG)

    def open_layers():
        with jax.named_scope("open_layers"):

            @pl.when(leader)
            def _():
                @pl.loop(0, REPLICAS - 1)
                def _(r):
                    pl.semaphore_signal(go_sem, inc=1, device_id=(r, fs), device_id_type=MESH)

            get_w.wait()
            frag[...] = jnp.where(
                lane_first > 0.5, w_now[:, :HEAD].astype(jnp.float32), w_now[:, HEAD:].astype(jnp.float32)
            ).astype(jnp.bfloat16)

    def layer_scatter():
        with jax.named_scope("layer_scatter"):

            @pl.when(jnp.logical_not(leader))
            def _():
                pl.semaphore_wait(go_sem, 1)

            return [
                remote(frag.at[segment(dx, dc)], layer_in.at[i], ls.at[i], lr.at[i], layer_dev(dx, dc))
                for i, (dx, dc) in enumerate(LAYER)
            ]

    width_scale = 1.0 / math.sqrt(D)
    token_scale = 1.0 / math.sqrt(TOK * FSDP)
    rcp, dcp = {}, {}

    def stage_raw(step, g):
        n = GROUPS[step][g]
        e = EXCH.index((step, g))
        with jax.named_scope(f"raw_{step}_{g}"):
            rsends[step, g][...] = jnp.dot(
                xbufs[step, g][...], w_now[...], preferred_element_type=jnp.float32
            ).astype(jnp.bfloat16)
            cps = []
            for i, o in enumerate(PLANE):
                cps.append(
                    remote(
                        rsends[step, g].at[pl.ds(slot(*o) * n, n)],
                        rrecvs[step, g].at[i],
                        rs.at[e, i],
                        rr.at[e, i],
                        plane_dev(*o),
                    )
                )
            rcp[step, g] = cps

    def stage_delta(step, g):
        n = GROUPS[step][g]
        e = EXCH.index((step, g))
        with jax.named_scope(f"wait_raw_{step}_{g}"):
            arrive(rcp[step, g], f"raw_{step}_{g}")
        with jax.named_scope(f"delta_{step}_{g}"):
            raw = rsends[step, g][:n].astype(jnp.float32)
            for i in range(len(PLANE)):
                raw = raw + rrecvs[step, g][i].astype(jnp.float32)
            raw = raw * width_scale
            up = cot[step, pl.ds(sum(GROUPS[step][:g]), n)].astype(jnp.float32)
            gain = gain_ref[...]
            for k in range(KV):
                cols = slice(k * HEAD, (k + 1) * HEAD)
                r = raw[:, cols]
                p = up[:, cols] * gain
                inv = lax.rsqrt(jnp.mean(r * r, axis=-1, keepdims=True) + norm_eps)
                dotp = jnp.mean(p * r, axis=-1, keepdims=True)
                dbufs[step, g][:n, cols] = (inv * p - r * (inv * inv * inv) * dotp).astype(jnp.bfloat16)
            cps = []
            for i, o in enumerate(PLANE):
                cps.append(
                    remote(
                        dbufs[step, g].at[pl.ds(0, n)],
                        dbufs[step, g].at[pl.ds(back(*o) * n, n)],
                        ds.at[e, i],
                        dr.at[e, i],
                        plane_dev(*o),
                    )
                )
            dcp[step, g] = cps

    def stage_grad(step, g, finish):
        with jax.named_scope(f"wait_delta_{step}_{g}"):
            arrive(dcp[step, g], f"delta_{step}_{g}")
        with jax.named_scope(f"grad_{step}_{g}"):
            d = dbufs[step, g][...]
            for t in range(ROWS // TILE):
                rows = pl.ds(t * TILE, TILE)
                acc = lax.dot_general(
                    xbufs[step, g][:, rows], d, (((0,), (0,)), ((), ())), preferred_element_type=jnp.float32
                )
                if g > 0:
                    acc = acc + grad[rows]
                if finish is None:
                    grad[rows] = acc
                else:
                    finish(rows, acc * token_scale)

    def adamw(rows, g):
        m = beta_first * m_now[rows] + (1.0 - beta_first) * g
        v = beta_second * v_now[rows] + (1.0 - beta_second) * g * g
        w = w_now[rows].astype(jnp.float32)
        w = w - inner_rate * (m / (jnp.sqrt(v) + adam_eps) + decay_rate * w)
        return w.astype(jnp.bfloat16), m, v

    def finish_first(rows, g):
        w, m, v = adamw(rows, g)
        w_now[rows] = w
        m_now[rows] = m
        v_now[rows] = v

    def finish_last(rows, g):
        w, _, _ = adamw(rows, g)
        mixed = newanchor[rows]
        for k in range(KV):
            cols = slice(k * HEAD, (k + 1) * HEAD)
            mine = w[:, cols].astype(jnp.float32)
            chosen = lane_first > 0.5 if k == 0 else lane_first < 0.5
            out_w[0, rows, cols] = jnp.where(
                chosen, mix_local * mine + (1.0 - mix_local) * mixed, mine
            ).astype(jnp.bfloat16)

    def layer_sum(layer_cps):
        with jax.named_scope("layer_sum"):
            arrive(layer_cps, "layer")
            s = frag[segment(0, 0)].astype(jnp.float32)
            for i in range(len(LAYER)):
                s = s + layer_in[i].astype(jnp.float32)
            partial[...] = s
            cps = []
            for i, dh in enumerate(LAYERS):
                where = pl.ds(pl.multiple_of(lax.rem(zh + dh, 4) * PIECE, 8), PIECE)
                cps.append(remote(partial.at[where], pieces.at[i], ps.at[i], pr.at[i], stack_dev(dh)))
            return cps

    def stack_sum(cps):
        with jax.named_scope("stack_sum"):
            arrive(cps, "stack_sum")
            s = partial[pl.ds(pl.multiple_of(zh * PIECE, 8), PIECE)]
            for i in range(len(LAYERS)):
                s = s + pieces[i]
            mine = pl.ds(pl.multiple_of(layer_index(0, 0) * SEG + zh * PIECE, 8), PIECE)
            total[mine] = s
            out = []
            for i, dh in enumerate(LAYERS):
                out.append(remote(total.at[mine], total.at[mine], qs.at[i], qr.at[i], stack_dev(dh)))
            return out

    def layer_gather(cps):
        with jax.named_scope("layer_gather"):
            arrive(cps, "layer_gather")
            out = []
            for i, (dx, dc) in enumerate(LAYER):
                out.append(
                    remote(
                        total.at[segment(0, 0)], total.at[segment(0, 0)], ts.at[i], tr.at[i], layer_dev(dx, dc)
                    )
                )
            return out

    def outer(cps):
        with jax.named_scope("outer"):
            arrive(cps, "outer")
            get_anchor.wait()
            get_mom.wait()
            a = anchor[...]
            mean = a - total[...] * (1.0 / REPLICAS)
            nm = outer_beta * mom[...] + mean
            newmom[...] = nm
            newanchor[...] = a - outer_rate * (mean + outer_beta * nm)

    held = {}

    def first_moments():
        get_m.wait()
        get_v.wait()

    def hold(name, value):
        held[name] = value

    todo = {
        48: [lambda: hold("scatter", layer_scatter())],
        64: [lambda: get_cot.wait(), lambda: stage_raw(0, 0)],
        96: [lambda: stage_delta(0, 0)],
        112: [lambda: hold("layer", layer_sum(held["scatter"]))],
        128: [lambda: stage_raw(0, 1), lambda: stage_grad(0, 0, None)],
        144: [lambda: hold("stack", stack_sum(held["layer"]))],
        160: [lambda: stage_delta(0, 1)],
        176: [lambda: hold("gather", layer_gather(held["stack"]))],
        192: [first_moments, lambda: stage_grad(0, 1, finish_first), lambda: stage_raw(1, 0)],
        208: [lambda: outer(held["gather"])],
        224: [lambda: stage_delta(1, 0)],
        240: [lambda: stage_raw(1, 1)],
        256: [
            lambda: stage_raw(1, 2),
            lambda: stage_grad(1, 0, None),
            lambda: stage_delta(1, 1),
            lambda: stage_delta(1, 2),
            lambda: stage_grad(1, 1, None),
            lambda: stage_grad(1, 2, finish_last),
        ],
    }
    open_layers()
    for k in range(len(UNITS)):
        landed(k)
        before = position
        position += UNITS[k][2]
        for mark in sorted(todo):
            if before < mark <= position:
                for act in todo[mark]:
                    act()
        top_up()
    with jax.named_scope("write"):
        for cp in sends:
            cp.wait_send()


def flush(a_ref, b_ref, c_ref, a_out, b_out, c_out, sems):
    cps = []
    n = ROWS // PARTS
    for k in range(PARTS):
        part = pl.ds(k * n, n)
        cps.append(pltpu.make_async_copy(a_ref.at[0, part], a_out.at[0, part], sems.at[0, k]))
        cps.append(pltpu.make_async_copy(b_ref.at[part], b_out.at[part], sems.at[1, k]))
        cps.append(pltpu.make_async_copy(c_ref.at[part], c_out.at[part], sems.at[2, k]))
    for cp in cps:
        cp.start()
    for cp in cps:
        cp.wait()


def body(layer_input, cotangent, weight, first_moment, second_moment, key_gain, frag_index, anchor, momentum):
    bf, f32 = jnp.bfloat16, jnp.float32
    dma = pltpu.SemaphoreType.DMA
    any_spec = pl.BlockSpec(memory_space=pltpu.HBM)
    sizes = [GROUPS[s][g] for s, g in EXCH]
    scratch = [pltpu.VMEM((FSDP * n, ROWS), bf) for n in sizes]
    scratch += [pltpu.VMEM((FSDP * n, C), bf) for n in sizes]
    scratch += [pltpu.VMEM((len(PLANE), n, C), bf) for n in sizes]
    scratch += [pltpu.VMEM((FSDP * n, C), bf) for n in sizes]
    scratch += [
        pltpu.VMEM((STEPS, TOK, C), bf),
        pltpu.VMEM((ROWS, C), bf),
        pltpu.VMEM((ROWS, C), f32),
        pltpu.VMEM((ROWS, C), f32),
        pltpu.VMEM((ROWS, C), f32),
        pltpu.VMEM((ROWS, HEAD), f32),
        pltpu.VMEM((ROWS, HEAD), f32),
        pltpu.VMEM((ROWS, HEAD), bf),
        pltpu.VMEM((len(LAYER), SEG, HEAD), bf),
        pltpu.VMEM((SEG, HEAD), f32),
        pltpu.VMEM((len(LAYERS), PIECE, HEAD), f32),
        pltpu.VMEM((ROWS, HEAD), f32),
        dma((6,)),
        dma((len(UNITS),)),
        dma((len(UNITS), 7)),
        dma((len(UNITS), 7)),
        dma((len(EXCH), 7)),
        dma((len(EXCH), 7)),
        dma((len(EXCH), 7)),
        dma((len(EXCH), 7)),
        dma((7,)),
        dma((7,)),
        dma((3,)),
        dma((3,)),
        dma((3,)),
        dma((3,)),
        dma((7,)),
        dma((7,)),
        pltpu.SemaphoreType.REGULAR,
    ]
    vmem_spec = pl.BlockSpec(memory_space=pltpu.VMEM)
    outs = pl.pallas_call(
        kernel,
        name="inner_outer",
        out_shape=(
            pltpu.VMEM((1, ROWS, C), bf),
            pltpu.VMEM((ROWS, HEAD), f32),
            pltpu.VMEM((ROWS, HEAD), f32),
        ),
        in_specs=[any_spec] * 5 + [vmem_spec, pl.BlockSpec(memory_space=pltpu.SMEM)] + [any_spec] * 2,
        out_specs=(vmem_spec, vmem_spec, vmem_spec),
        scratch_shapes=scratch,
        compiler_params=pltpu.CompilerParams(
            collective_id=0, has_side_effects=True, vmem_limit_bytes=LIMIT
        ),
    )(
        layer_input, cotangent, weight, first_moment, second_moment,
        key_gain.reshape(1, HEAD), frag_index, anchor, momentum,
    )
    return outs


def solution(mesh):
    placed = (
        P("replica", None, "fsdp", None),
        P("replica", None, "fsdp", None),
        P("replica", "fsdp", None),
        P("replica", "fsdp", None),
        P("replica", "fsdp", None),
        P(),
        P(),
        P("fsdp", None),
        P("fsdp", None),
    )
    return jax.shard_map(
        body,
        mesh=mesh,
        in_specs=placed,
        out_specs=(P("replica", "fsdp", None), P("fsdp", None), P("fsdp", None)),
        check_vma=False,
    )
```

```python
import math

import jax
import jax.numpy as jnp
from jax import lax
from jax.experimental import pallas as pl
from jax.experimental.pallas import tpu as pltpu
from jax.sharding import PartitionSpec as P

D = 12288
HEAD = 128
KV = 2
C = KV * HEAD
TOK = 128
STEPS = 2
FSDP = 8
ROWS = D // FSDP
REPLICAS = 32
GROUPS = ((80, 48), (64, 48, 16))
STAGED = ((0, 0),)
ROW = ((0, 1), (0, 3), (0, 2))
PLAN = (
    (48, "scatter", 0, 0),
    (80, "raw", 0, 0),
    (96, "fold", 0, 0),
    (112, "layer", 0, 0),
    (112, "delta", 0, 0),
    (128, "pass", 0, 0),
    (128, "raw", 0, 1),
    (144, "stack", 0, 0),
    (160, "delta", 0, 1),
    (160, "grad", 0, 0),
    (176, "gather", 0, 0),
    (176, "grad", 0, 1),
    (192, "raw", 1, 0),
    (208, "outer", 0, 0),
    (224, "delta", 1, 0),
    (240, "raw", 1, 1),
    (256, "raw", 1, 2),
    (256, "grad", 1, 0),
    (256, "delta", 1, 1),
    (256, "delta", 1, 2),
    (256, "grad", 1, 1),
    (256, "grad", 1, 2),
)
SIZES = ((16,) * 8, (16,) * 8)
AHEAD = 48
UNITS = tuple((s, sum(SIZES[s][:i]), n) for s in range(STEPS) for i, n in enumerate(SIZES[s]))
EXCH = tuple((s, g) for s in range(STEPS) for g in range(len(GROUPS[s])))
TILE = 256
PARTS = 2
LIMIT = 61 << 20

beta_first = 0.9
beta_second = 0.95
inner_rate = 2.0
decay_rate = 0.05
adam_eps = 1e-08
norm_eps = 1e-06
outer_rate = 0.7
outer_beta = 0.9
mix_local = 0.5

PLANE = ((1, 2), (0, 2), (1, 1), (1, 3), (0, 1), (0, 3), (1, 0))
LAYER = tuple((dx, dc) for dx in (2, 1, 3, 0) for dc in (0, 1) if (dx, dc) != (0, 0))
LAYERS = (2, 1, 3)
SEG = ROWS // 8
PIECE = SEG // 4
MESH = pl.DeviceIdType.MESH


def kernel(
    x_hbm, cot_hbm, w_hbm, m_hbm, v_hbm, gain_ref, frag_ref, anchor_hbm, mom_hbm,
    out_w, newmom, newanchor,
    *scratch,
):
    count = len(EXCH)
    xbufs = dict(zip(EXCH, scratch[:count]))
    rsends = dict(zip(EXCH, scratch[count : 2 * count]))
    rrecvs = dict(zip(EXCH, scratch[2 * count : 3 * count]))
    dbufs = dict(zip(EXCH, scratch[3 * count : 4 * count]))
    split = 4 * count + len(STAGED)
    zrecvs = dict(zip(STAGED, scratch[4 * count : split]))
    folds = dict(zip(STAGED, scratch[split : split + len(STAGED)]))
    (
        cot, w_now, m_now, v_now, grad, anchor, mom, frag, layer_in, partial, pieces, total,
        loc_sem, own_sem, xs, xr, rs, rr, ds, dr, ls, lr, ps, pr, qs, qr, ts, tr, zs, zr, go_sem,
    ) = scratch[split + len(STAGED) :]
    rep = lax.axis_index("replica")
    fs = lax.axis_index("fsdp")
    zl, yy = fs // 4, lax.rem(fs, 4)
    zh, xx, cc = rep // 8, lax.rem(rep // 2, 4), lax.rem(rep, 2)

    def plane_index(dz, dy):
        return lax.rem(zl + dz, 2) * 4 + lax.rem(yy + dy, 4)

    def layer_index(dx, dc):
        return lax.rem(xx + dx, 4) * 2 + lax.rem(cc + dc, 2)

    def plane_dev(dz, dy):
        return (rep, plane_index(dz, dy))

    def layer_dev(dx, dc):
        return (zh * 8 + layer_index(dx, dc), fs)

    def stack_dev(dh):
        return (lax.rem(zh + dh, 4) * 8 + xx * 2 + cc, fs)

    leader = rep == REPLICAS - 1
    with jax.named_scope("entry"):
        bar = pltpu.get_barrier_semaphore()
        for o in PLANE:
            pl.semaphore_signal(bar, inc=1, device_id=plane_dev(*o), device_id_type=MESH)

        @pl.when(jnp.logical_not(leader))
        def _():
            pl.semaphore_signal(bar, inc=1, device_id=(REPLICAS - 1, fs), device_id_type=MESH)
            pl.semaphore_wait(bar, len(PLANE))

        @pl.when(leader)
        def _():
            pl.semaphore_wait(bar, len(PLANE) + REPLICAS - 1)

    sends = []

    def remote(src, dst, s, r, dev):
        cp = pltpu.make_async_remote_copy(
            src_ref=src, dst_ref=dst, send_sem=s, recv_sem=r, device_id=dev, device_id_type=MESH
        )
        cp.start()
        sends.append(cp)
        return cp

    def arrive(cps, name):
        for cp in cps:
            cp.wait_recv()

    def slot(dz, dy):
        return dz * 4 + dy

    def back(dz, dy):
        return dz * 4 + (4 - dy) % 4

    def columns(dz, dy):
        return pl.ds(pl.multiple_of(plane_index(dz, dy) * ROWS, 128), ROWS)

    def place(step, row):
        g = 0
        while row >= GROUPS[step][g]:
            row -= GROUPS[step][g]
            g += 1
        return g, row

    def send_x(k):
        step, row, rows = UNITS[k]
        g, at = place(step, row)
        n = GROUPS[step][g]
        got = []
        for i, o in enumerate(PLANE):
            got.append(
                remote(
                    x_hbm.at[0, step, pl.ds(row, rows), columns(*o)],
                    xbufs[step, g].at[pl.ds(back(*o) * n + at, rows)],
                    xs.at[k, i],
                    xr.at[k, i],
                    plane_dev(*o),
                )
            )
        own = pltpu.make_async_copy(
            x_hbm.at[0, step, pl.ds(row, rows), columns(0, 0)],
            xbufs[step, g].at[pl.ds(at, rows)],
            own_sem.at[k],
        )
        own.start()
        return got, own

    def local(src, dst, i):
        cp = pltpu.make_async_copy(src, dst, loc_sem.at[i])
        cp.start()
        return cp

    xcp = {}

    def issue(k):
        if k < len(UNITS):
            with jax.named_scope("send_x"):
                xcp[k] = send_x(k)

    def landed(k):
        with jax.named_scope("wait_x"):
            got, own = xcp[k]
            own.wait()
            arrive(got, f"x_{k}")

    issued = 0
    done = 0
    position = 0

    def top_up():
        nonlocal issued, done
        while issued < len(UNITS) and (issued == 0 or sum(u[2] for u in UNITS[:issued]) < position + AHEAD):
            issue(issued)
            issued += 1

    top_up()
    get_w = local(w_hbm.at[0], w_now, 0)
    get_cot = local(cot_hbm.at[0], cot, 1)
    get_m = local(m_hbm.at[0], m_now, 2)
    get_v = local(v_hbm.at[0], v_now, 3)
    get_anchor = local(anchor_hbm, anchor, 4)
    get_mom = local(mom_hbm, mom, 5)

    first_frag = lax.rem(frag_ref[0], KV) == 0
    lane_first = jnp.where(first_frag, jnp.float32(1.0), jnp.float32(0.0))

    def segment(dx, dc):
        return pl.ds(pl.multiple_of(layer_index(dx, dc) * SEG, 16), SEG)

    def open_layers():
        with jax.named_scope("open_layers"):

            @pl.when(leader)
            def _():
                @pl.loop(0, REPLICAS - 1)
                def _(r):
                    pl.semaphore_signal(go_sem, inc=1, device_id=(r, fs), device_id_type=MESH)

            get_w.wait()
            frag[...] = jnp.where(
                lane_first > 0.5, w_now[:, :HEAD].astype(jnp.float32), w_now[:, HEAD:].astype(jnp.float32)
            ).astype(jnp.bfloat16)

    def layer_scatter():
        with jax.named_scope("layer_scatter"):

            @pl.when(jnp.logical_not(leader))
            def _():
                pl.semaphore_wait(go_sem, 1)

            return [
                remote(frag.at[segment(dx, dc)], layer_in.at[i], ls.at[i], lr.at[i], layer_dev(dx, dc))
                for i, (dx, dc) in enumerate(LAYER)
            ]

    width_scale = 1.0 / math.sqrt(D)
    token_scale = 1.0 / math.sqrt(TOK * FSDP)
    rcp, dcp = {}, {}
    mcp, zcp, fcp = {}, {}, {}

    def stage_raw(step, g):
        n = GROUPS[step][g]
        e = EXCH.index((step, g))
        with jax.named_scope(f"raw_{step}_{g}"):
            rsends[step, g][...] = jnp.dot(
                xbufs[step, g][...], w_now[...], preferred_element_type=jnp.float32
            ).astype(jnp.bfloat16)
            if (step, g) in STAGED:
                mcp[step, g] = [
                    remote(
                        rsends[step, g].at[pl.ds(4 * n, 4 * n)],
                        zrecvs[step, g],
                        zs.at[e],
                        zr.at[e],
                        plane_dev(1, 0),
                    )
                ]
                return
            rcp[step, g] = [
                remote(
                    rsends[step, g].at[pl.ds(slot(*o) * n, n)],
                    rrecvs[step, g].at[i],
                    rs.at[e, i],
                    rr.at[e, i],
                    plane_dev(*o),
                )
                for i, o in enumerate(PLANE)
            ]

    def stage_fold(step, g):
        n = GROUPS[step][g]
        e = EXCH.index((step, g))
        with jax.named_scope(f"fold_{step}_{g}"):
            arrive(mcp[step, g], f"fold_{step}_{g}")
            folds[step, g][...] = (
                rsends[step, g][: 4 * n].astype(jnp.float32) + zrecvs[step, g][...].astype(jnp.float32)
            ).astype(jnp.bfloat16)
            rcp[step, g] = [
                remote(
                    folds[step, g].at[pl.ds(dy * n, n)],
                    rrecvs[step, g].at[i],
                    rs.at[e, i],
                    rr.at[e, i],
                    plane_dev(0, dy),
                )
                for i, (_, dy) in enumerate(ROW)
            ]

    def stage_delta(step, g):
        n = GROUPS[step][g]
        e = EXCH.index((step, g))
        staged = (step, g) in STAGED
        with jax.named_scope(f"wait_raw_{step}_{g}"):
            arrive(rcp[step, g], f"raw_{step}_{g}")
        with jax.named_scope(f"delta_{step}_{g}"):
            mine = folds[step, g] if staged else rsends[step, g]
            raw = mine[:n].astype(jnp.float32)
            for i in range(len(rcp[step, g])):
                raw = raw + rrecvs[step, g][i].astype(jnp.float32)
            raw = raw * width_scale
            up = cot[step, pl.ds(sum(GROUPS[step][:g]), n)].astype(jnp.float32)
            gain = gain_ref[...]
            for k in range(KV):
                cols = slice(k * HEAD, (k + 1) * HEAD)
                r = raw[:, cols]
                p = up[:, cols] * gain
                inv = lax.rsqrt(jnp.mean(r * r, axis=-1, keepdims=True) + norm_eps)
                dotp = jnp.mean(p * r, axis=-1, keepdims=True)
                dbufs[step, g][:n, cols] = (inv * p - r * (inv * inv * inv) * dotp).astype(jnp.bfloat16)
            targets = ((1, 0),) + ROW if staged else PLANE
            cps = [
                remote(
                    dbufs[step, g].at[pl.ds(0, n)],
                    dbufs[step, g].at[pl.ds(back(*o) * n, n)],
                    ds.at[e, i],
                    dr.at[e, i],
                    plane_dev(*o),
                )
                for i, o in enumerate(targets)
            ]
            if staged:
                zcp[step, g], cps = cps[:1], cps[1:]
            dcp[step, g] = cps

    def stage_pass(step, g):
        n = GROUPS[step][g]
        e = EXCH.index((step, g))
        with jax.named_scope(f"pass_{step}_{g}"):
            arrive(zcp[step, g], f"pass_{step}_{g}")
            dcp[step, g] = dcp[step, g] + [
                remote(
                    dbufs[step, g].at[pl.ds(4 * n, n)],
                    dbufs[step, g].at[pl.ds((4 + back(0, dy)) * n, n)],
                    ds.at[e, 4 + i],
                    dr.at[e, 4 + i],
                    plane_dev(0, dy),
                )
                for i, (_, dy) in enumerate(ROW)
            ]

    def stage_grad(step, g, finish):
        with jax.named_scope(f"wait_delta_{step}_{g}"):
            arrive(dcp[step, g], f"delta_{step}_{g}")
        with jax.named_scope(f"grad_{step}_{g}"):
            d = dbufs[step, g][...]
            for t in range(ROWS // TILE):
                rows = pl.ds(t * TILE, TILE)
                acc = lax.dot_general(
                    xbufs[step, g][:, rows], d, (((0,), (0,)), ((), ())), preferred_element_type=jnp.float32
                )
                if g > 0:
                    acc = acc + grad[rows]
                if finish is None:
                    grad[rows] = acc
                else:
                    finish(rows, acc * token_scale)

    def adamw(rows, g):
        m = beta_first * m_now[rows] + (1.0 - beta_first) * g
        v = beta_second * v_now[rows] + (1.0 - beta_second) * g * g
        w = w_now[rows].astype(jnp.float32)
        w = w - inner_rate * (m / (jnp.sqrt(v) + adam_eps) + decay_rate * w)
        return w.astype(jnp.bfloat16), m, v

    def finish_first(rows, g):
        w, m, v = adamw(rows, g)
        w_now[rows] = w
        m_now[rows] = m
        v_now[rows] = v

    def finish_last(rows, g):
        w, _, _ = adamw(rows, g)
        mixed = newanchor[rows]
        for k in range(KV):
            cols = slice(k * HEAD, (k + 1) * HEAD)
            mine = w[:, cols].astype(jnp.float32)
            chosen = lane_first > 0.5 if k == 0 else lane_first < 0.5
            out_w[0, rows, cols] = jnp.where(
                chosen, mix_local * mine + (1.0 - mix_local) * mixed, mine
            ).astype(jnp.bfloat16)

    def layer_sum(layer_cps):
        with jax.named_scope("layer_sum"):
            arrive(layer_cps, "layer")
            s = frag[segment(0, 0)].astype(jnp.float32)
            for i in range(len(LAYER)):
                s = s + layer_in[i].astype(jnp.float32)
            partial[...] = s
            cps = []
            for i, dh in enumerate(LAYERS):
                where = pl.ds(pl.multiple_of(lax.rem(zh + dh, 4) * PIECE, 8), PIECE)
                cps.append(remote(partial.at[where], pieces.at[i], ps.at[i], pr.at[i], stack_dev(dh)))
            return cps

    def stack_sum(cps):
        with jax.named_scope("stack_sum"):
            arrive(cps, "stack_sum")
            s = partial[pl.ds(pl.multiple_of(zh * PIECE, 8), PIECE)]
            for i in range(len(LAYERS)):
                s = s + pieces[i]
            mine = pl.ds(pl.multiple_of(layer_index(0, 0) * SEG + zh * PIECE, 8), PIECE)
            total[mine] = s
            out = []
            for i, dh in enumerate(LAYERS):
                out.append(remote(total.at[mine], total.at[mine], qs.at[i], qr.at[i], stack_dev(dh)))
            return out

    def layer_gather(cps):
        with jax.named_scope("layer_gather"):
            arrive(cps, "layer_gather")
            out = []
            for i, (dx, dc) in enumerate(LAYER):
                out.append(
                    remote(
                        total.at[segment(0, 0)], total.at[segment(0, 0)], ts.at[i], tr.at[i], layer_dev(dx, dc)
                    )
                )
            return out

    def outer(cps):
        with jax.named_scope("outer"):
            arrive(cps, "outer")
            get_anchor.wait()
            get_mom.wait()
            a = anchor[...]
            mean = a - total[...] * (1.0 / REPLICAS)
            nm = outer_beta * mom[...] + mean
            newmom[...] = nm
            newanchor[...] = a - outer_rate * (mean + outer_beta * nm)

    held = {}

    def act(kind, step, g):
        if kind == "raw":
            stage_raw(step, g)
        elif kind == "fold":
            stage_fold(step, g)
        elif kind == "delta":
            stage_delta(step, g)
        elif kind == "pass":
            stage_pass(step, g)
        elif kind == "grad":
            final = g == len(GROUPS[step]) - 1
            if final and step == 0:
                get_m.wait()
                get_v.wait()
            stage_grad(step, g, (finish_first, finish_last)[step] if final else None)
        elif kind == "scatter":
            held["sent"] = layer_scatter()
        elif kind == "layer":
            held["sent"] = layer_sum(held["sent"])
        elif kind == "stack":
            held["sent"] = stack_sum(held["sent"])
        elif kind == "gather":
            held["sent"] = layer_gather(held["sent"])
        elif kind == "outer":
            outer(held["sent"])

    open_layers()
    get_cot.wait()
    for k in range(len(UNITS)):
        landed(k)
        before = position
        position += UNITS[k][2]
        for mark, *what in PLAN:
            if before < mark <= position:
                act(*what)
        top_up()
    with jax.named_scope("write"):
        for cp in sends:
            cp.wait_send()


def flush(a_ref, b_ref, c_ref, a_out, b_out, c_out, sems):
    cps = []
    n = ROWS // PARTS
    for k in range(PARTS):
        part = pl.ds(k * n, n)
        cps.append(pltpu.make_async_copy(a_ref.at[0, part], a_out.at[0, part], sems.at[0, k]))
        cps.append(pltpu.make_async_copy(b_ref.at[part], b_out.at[part], sems.at[1, k]))
        cps.append(pltpu.make_async_copy(c_ref.at[part], c_out.at[part], sems.at[2, k]))
    for cp in cps:
        cp.start()
    for cp in cps:
        cp.wait()


def body(layer_input, cotangent, weight, first_moment, second_moment, key_gain, frag_index, anchor, momentum):
    bf, f32 = jnp.bfloat16, jnp.float32
    dma = pltpu.SemaphoreType.DMA
    any_spec = pl.BlockSpec(memory_space=pltpu.HBM)
    sizes = [GROUPS[s][g] for s, g in EXCH]
    scratch = [pltpu.VMEM((FSDP * n, ROWS), bf) for n in sizes]
    scratch += [pltpu.VMEM((FSDP * n, C), bf) for n in sizes]
    scratch += [pltpu.VMEM((3 if e in STAGED else 7, GROUPS[e[0]][e[1]], C), bf) for e in EXCH]
    scratch += [pltpu.VMEM((FSDP * n, C), bf) for n in sizes]
    scratch += [pltpu.VMEM((4 * GROUPS[s][g], C), bf) for s, g in STAGED] * 2
    scratch += [
        pltpu.VMEM((STEPS, TOK, C), bf),
        pltpu.VMEM((ROWS, C), bf),
        pltpu.VMEM((ROWS, C), f32),
        pltpu.VMEM((ROWS, C), f32),
        pltpu.VMEM((ROWS, C), f32),
        pltpu.VMEM((ROWS, HEAD), f32),
        pltpu.VMEM((ROWS, HEAD), f32),
        pltpu.VMEM((ROWS, HEAD), bf),
        pltpu.VMEM((len(LAYER), SEG, HEAD), bf),
        pltpu.VMEM((SEG, HEAD), f32),
        pltpu.VMEM((len(LAYERS), PIECE, HEAD), f32),
        pltpu.VMEM((ROWS, HEAD), f32),
        dma((6,)),
        dma((len(UNITS),)),
        dma((len(UNITS), 7)),
        dma((len(UNITS), 7)),
        dma((len(EXCH), 7)),
        dma((len(EXCH), 7)),
        dma((len(EXCH), 7)),
        dma((len(EXCH), 7)),
        dma((7,)),
        dma((7,)),
        dma((3,)),
        dma((3,)),
        dma((3,)),
        dma((3,)),
        dma((7,)),
        dma((7,)),
        dma((len(EXCH),)),
        dma((len(EXCH),)),
        pltpu.SemaphoreType.REGULAR,
    ]
    vmem_spec = pl.BlockSpec(memory_space=pltpu.VMEM)
    outs = pl.pallas_call(
        kernel,
        name="inner_outer",
        out_shape=(
            pltpu.VMEM((1, ROWS, C), bf),
            pltpu.VMEM((ROWS, HEAD), f32),
            pltpu.VMEM((ROWS, HEAD), f32),
        ),
        in_specs=[any_spec] * 5 + [vmem_spec, pl.BlockSpec(memory_space=pltpu.SMEM)] + [any_spec] * 2,
        out_specs=(vmem_spec, vmem_spec, vmem_spec),
        scratch_shapes=scratch,
        compiler_params=pltpu.CompilerParams(
            collective_id=0, has_side_effects=True, vmem_limit_bytes=LIMIT
        ),
    )(
        layer_input, cotangent, weight, first_moment, second_moment,
        key_gain.reshape(1, HEAD), frag_index, anchor, momentum,
    )
    outs = [pltpu.with_memory_space_constraint(o, pltpu.VMEM) for o in outs]
    return pl.pallas_call(
        flush,
        name="flush",
        out_shape=[jax.ShapeDtypeStruct(o.shape, o.dtype) for o in outs],
        in_specs=[vmem_spec] * 3,
        out_specs=[any_spec] * 3,
        scratch_shapes=[dma((3, PARTS))],
        compiler_params=pltpu.CompilerParams(vmem_limit_bytes=1 << 20),
    )(*outs)


def solution(mesh):
    placed = (
        P("replica", None, "fsdp", None),
        P("replica", None, "fsdp", None),
        P("replica", "fsdp", None),
        P("replica", "fsdp", None),
        P("replica", "fsdp", None),
        P(),
        P(),
        P("fsdp", None),
        P("fsdp", None),
    )
    return jax.shard_map(
        body,
        mesh=mesh,
        in_specs=placed,
        out_specs=(P("replica", "fsdp", None), P("fsdp", None), P("fsdp", None)),
        check_vma=False,
    )
```

```python
import math

import jax
import jax.numpy as jnp
from jax import lax
from jax.experimental import pallas as pl
from jax.experimental.pallas import tpu as pltpu
from jax.sharding import PartitionSpec as P

D = 12288
HEAD = 128
KV = 2
C = KV * HEAD
TOK = 128
STEPS = 2
FSDP = 8
ROWS = D // FSDP
REPLICAS = 32
GROUPS = ((80, 48), (64, 48, 16))
STAGED = ()
YFIRST = ((0, 0),)
PASSED = ((0, 0),)
ROW = ((0, 1), (0, 3), (0, 2))
PLAN = (
    (48, "scatter", 0, 0),
    (80, "raw", 0, 0),
    (112, "layer", 0, 0),
    (112, "fold", 0, 0),
    (128, "delta", 0, 0),
    (128, "raw", 0, 1),
    (144, "stack", 0, 0),
    (160, "pass", 0, 0),
    (160, "delta", 0, 1),
    (176, "gather", 0, 0),
    (176, "grad", 0, 0),
    (192, "grad", 0, 1),
    (192, "raw", 1, 0),
    (208, "outer", 0, 0),
    (224, "delta", 1, 0),
    (240, "raw", 1, 1),
    (256, "raw", 1, 2),
    (256, "delta", 1, 1),
    (256, "grad", 1, 0),
    (256, "delta", 1, 2),
    (256, "grad", 1, 1),
    (256, "grad", 1, 2),
)
SIZES = ((16,) * 8, (16,) * 8)
AHEAD = 48
UNITS = tuple((s, sum(SIZES[s][:i]), n) for s in range(STEPS) for i, n in enumerate(SIZES[s]))
EXCH = tuple((s, g) for s in range(STEPS) for g in range(len(GROUPS[s])))
TILE = 256
PARTS = 2
LIMIT = 61 << 20

beta_first = 0.9
beta_second = 0.95
inner_rate = 2.0
decay_rate = 0.05
adam_eps = 1e-08
norm_eps = 1e-06
outer_rate = 0.7
outer_beta = 0.9
mix_local = 0.5

PLANE = ((1, 2), (0, 2), (1, 1), (1, 3), (0, 1), (0, 3), (1, 0))
LAYER = tuple((dx, dc) for dx in (2, 1, 3, 0) for dc in (0, 1) if (dx, dc) != (0, 0))
LAYERS = (2, 1, 3)
SEG = ROWS // 8
PIECE = SEG // 4
MESH = pl.DeviceIdType.MESH


def kernel(
    x_hbm, cot_hbm, w_hbm, m_hbm, v_hbm, gain_ref, frag_ref, anchor_hbm, mom_hbm,
    out_w, newmom, newanchor,
    *scratch,
):
    count = len(EXCH)
    xbufs = dict(zip(EXCH, scratch[:count]))
    rsends = dict(zip(EXCH, scratch[count : 2 * count]))
    rrecvs = dict(zip(EXCH, scratch[2 * count : 3 * count]))
    dbufs = dict(zip(EXCH, scratch[3 * count : 4 * count]))
    both = STAGED + YFIRST
    split = 4 * count + len(both)
    zrecvs = dict(zip(both, scratch[4 * count : split]))
    folds = dict(zip(both, scratch[split : split + len(both)]))
    (
        cot, w_now, m_now, v_now, grad, anchor, mom, frag, layer_in, partial, pieces, total,
        loc_sem, own_sem, xs, xr, rs, rr, ds, dr, ls, lr, ps, pr, qs, qr, ts, tr, zs, zr, go_sem,
    ) = scratch[split + len(both) :]
    rep = lax.axis_index("replica")
    fs = lax.axis_index("fsdp")
    zl, yy = fs // 4, lax.rem(fs, 4)
    zh, xx, cc = rep // 8, lax.rem(rep // 2, 4), lax.rem(rep, 2)

    def plane_index(dz, dy):
        return lax.rem(zl + dz, 2) * 4 + lax.rem(yy + dy, 4)

    def layer_index(dx, dc):
        return lax.rem(xx + dx, 4) * 2 + lax.rem(cc + dc, 2)

    def plane_dev(dz, dy):
        return (rep, plane_index(dz, dy))

    def layer_dev(dx, dc):
        return (zh * 8 + layer_index(dx, dc), fs)

    def stack_dev(dh):
        return (lax.rem(zh + dh, 4) * 8 + xx * 2 + cc, fs)

    leader = rep == REPLICAS - 1
    with jax.named_scope("entry"):
        bar = pltpu.get_barrier_semaphore()
        for o in PLANE:
            pl.semaphore_signal(bar, inc=1, device_id=plane_dev(*o), device_id_type=MESH)

        @pl.when(jnp.logical_not(leader))
        def _():
            pl.semaphore_signal(bar, inc=1, device_id=(REPLICAS - 1, fs), device_id_type=MESH)
            pl.semaphore_wait(bar, len(PLANE))

        @pl.when(leader)
        def _():
            pl.semaphore_wait(bar, len(PLANE) + REPLICAS - 1)

    sends = []

    def remote(src, dst, s, r, dev):
        cp = pltpu.make_async_remote_copy(
            src_ref=src, dst_ref=dst, send_sem=s, recv_sem=r, device_id=dev, device_id_type=MESH
        )
        cp.start()
        sends.append(cp)
        return cp

    def arrive(cps, name):
        for cp in cps:
            cp.wait_recv()

    def slot(dz, dy):
        return dz * 4 + dy

    def back(dz, dy):
        return dz * 4 + (4 - dy) % 4

    def columns(dz, dy):
        return pl.ds(pl.multiple_of(plane_index(dz, dy) * ROWS, 128), ROWS)

    def place(step, row):
        g = 0
        while row >= GROUPS[step][g]:
            row -= GROUPS[step][g]
            g += 1
        return g, row

    def send_x(k):
        step, row, rows = UNITS[k]
        g, at = place(step, row)
        n = GROUPS[step][g]
        got = []
        for i, o in enumerate(PLANE):
            got.append(
                remote(
                    x_hbm.at[0, step, pl.ds(row, rows), columns(*o)],
                    xbufs[step, g].at[pl.ds(back(*o) * n + at, rows)],
                    xs.at[k, i],
                    xr.at[k, i],
                    plane_dev(*o),
                )
            )
        own = pltpu.make_async_copy(
            x_hbm.at[0, step, pl.ds(row, rows), columns(0, 0)],
            xbufs[step, g].at[pl.ds(at, rows)],
            own_sem.at[k],
        )
        own.start()
        return got, own

    def local(src, dst, i):
        cp = pltpu.make_async_copy(src, dst, loc_sem.at[i])
        cp.start()
        return cp

    xcp = {}

    def issue(k):
        if k < len(UNITS):
            with jax.named_scope("send_x"):
                xcp[k] = send_x(k)

    def landed(k):
        with jax.named_scope("wait_x"):
            got, own = xcp[k]
            own.wait()
            arrive(got, f"x_{k}")

    issued = 0
    done = 0
    position = 0

    def top_up():
        nonlocal issued, done
        while issued < len(UNITS) and (issued == 0 or sum(u[2] for u in UNITS[:issued]) < position + AHEAD):
            issue(issued)
            issued += 1

    top_up()
    get_w = local(w_hbm.at[0], w_now, 0)
    get_cot = local(cot_hbm.at[0], cot, 1)
    get_m = local(m_hbm.at[0], m_now, 2)
    get_v = local(v_hbm.at[0], v_now, 3)
    get_anchor = local(anchor_hbm, anchor, 4)
    get_mom = local(mom_hbm, mom, 5)

    first_frag = lax.rem(frag_ref[0], KV) == 0
    lane_first = jnp.where(first_frag, jnp.float32(1.0), jnp.float32(0.0))

    def segment(dx, dc):
        return pl.ds(pl.multiple_of(layer_index(dx, dc) * SEG, 16), SEG)

    def open_layers():
        with jax.named_scope("open_layers"):

            @pl.when(leader)
            def _():
                @pl.loop(0, REPLICAS - 1)
                def _(r):
                    pl.semaphore_signal(go_sem, inc=1, device_id=(r, fs), device_id_type=MESH)

            get_w.wait()
            frag[...] = jnp.where(
                lane_first > 0.5, w_now[:, :HEAD].astype(jnp.float32), w_now[:, HEAD:].astype(jnp.float32)
            ).astype(jnp.bfloat16)

    def layer_scatter():
        with jax.named_scope("layer_scatter"):

            @pl.when(jnp.logical_not(leader))
            def _():
                pl.semaphore_wait(go_sem, 1)

            return [
                remote(frag.at[segment(dx, dc)], layer_in.at[i], ls.at[i], lr.at[i], layer_dev(dx, dc))
                for i, (dx, dc) in enumerate(LAYER)
            ]

    width_scale = 1.0 / math.sqrt(D)
    token_scale = 1.0 / math.sqrt(TOK * FSDP)
    rcp, dcp = {}, {}
    mcp, zcp, fcp = {}, {}, {}

    def stage_raw(step, g):
        n = GROUPS[step][g]
        e = EXCH.index((step, g))
        with jax.named_scope(f"raw_{step}_{g}"):
            rsends[step, g][...] = jnp.dot(
                xbufs[step, g][...], w_now[...], preferred_element_type=jnp.float32
            ).astype(jnp.bfloat16)
            if (step, g) in STAGED:
                mcp[step, g] = [
                    remote(
                        rsends[step, g].at[pl.ds(4 * n, 4 * n)],
                        zrecvs[step, g],
                        zs.at[e],
                        zr.at[e],
                        plane_dev(1, 0),
                    )
                ]
                return
            if (step, g) in YFIRST:
                mcp[step, g] = [
                    remote(
                        rsends[step, g].at[pl.ds((4 * half + dy) * n, n)],
                        rrecvs[step, g].at[i, pl.ds(half * n, n)],
                        rs.at[e, 2 * i + half],
                        rr.at[e, 2 * i + half],
                        plane_dev(0, dy),
                    )
                    for i, (_, dy) in enumerate(ROW)
                    for half in range(2)
                ]
                return
            rcp[step, g] = [
                remote(
                    rsends[step, g].at[pl.ds(slot(*o) * n, n)],
                    rrecvs[step, g].at[i],
                    rs.at[e, i],
                    rr.at[e, i],
                    plane_dev(*o),
                )
                for i, o in enumerate(PLANE)
            ]

    def stage_fold(step, g):
        n = GROUPS[step][g]
        e = EXCH.index((step, g))
        with jax.named_scope(f"fold_{step}_{g}"):
            arrive(mcp[step, g], f"fold_{step}_{g}")
            if (step, g) in YFIRST:
                for half in range(2):
                    total_half = rsends[step, g][4 * half * n : (4 * half + 1) * n].astype(jnp.float32)
                    for i in range(len(ROW)):
                        total_half = total_half + rrecvs[step, g][i, half * n : (half + 1) * n].astype(jnp.float32)
                    folds[step, g][half * n : (half + 1) * n] = total_half.astype(jnp.bfloat16)
                rcp[step, g] = [
                    remote(
                        folds[step, g].at[pl.ds(n, n)], zrecvs[step, g], zs.at[e], zr.at[e], plane_dev(1, 0)
                    )
                ]
                return
            folds[step, g][...] = (
                rsends[step, g][: 4 * n].astype(jnp.float32) + zrecvs[step, g][...].astype(jnp.float32)
            ).astype(jnp.bfloat16)
            rcp[step, g] = [
                remote(
                    folds[step, g].at[pl.ds(dy * n, n)],
                    rrecvs[step, g].at[i],
                    rs.at[e, i],
                    rr.at[e, i],
                    plane_dev(0, dy),
                )
                for i, (_, dy) in enumerate(ROW)
            ]

    def stage_delta(step, g):
        n = GROUPS[step][g]
        e = EXCH.index((step, g))
        staged = (step, g) in STAGED
        yfirst = (step, g) in YFIRST
        passed = (step, g) in PASSED
        with jax.named_scope(f"wait_raw_{step}_{g}"):
            arrive(rcp[step, g], f"raw_{step}_{g}")
        with jax.named_scope(f"delta_{step}_{g}"):
            mine = folds[step, g] if staged or yfirst else rsends[step, g]
            raw = mine[:n].astype(jnp.float32)
            if yfirst:
                raw = raw + zrecvs[step, g][...].astype(jnp.float32)
            else:
                for i in range(len(rcp[step, g])):
                    raw = raw + rrecvs[step, g][i].astype(jnp.float32)
            raw = raw * width_scale
            up = cot[step, pl.ds(sum(GROUPS[step][:g]), n)].astype(jnp.float32)
            gain = gain_ref[...]
            for k in range(KV):
                cols = slice(k * HEAD, (k + 1) * HEAD)
                r = raw[:, cols]
                p = up[:, cols] * gain
                inv = lax.rsqrt(jnp.mean(r * r, axis=-1, keepdims=True) + norm_eps)
                dotp = jnp.mean(p * r, axis=-1, keepdims=True)
                dbufs[step, g][:n, cols] = (inv * p - r * (inv * inv * inv) * dotp).astype(jnp.bfloat16)
            targets = ((1, 0),) + ROW if passed else PLANE
            cps = [
                remote(
                    dbufs[step, g].at[pl.ds(0, n)],
                    dbufs[step, g].at[pl.ds(back(*o) * n, n)],
                    ds.at[e, i],
                    dr.at[e, i],
                    plane_dev(*o),
                )
                for i, o in enumerate(targets)
            ]
            if passed:
                zcp[step, g], cps = cps[:1], cps[1:]
            dcp[step, g] = cps

    def stage_pass(step, g):
        n = GROUPS[step][g]
        e = EXCH.index((step, g))
        with jax.named_scope(f"pass_{step}_{g}"):
            arrive(zcp[step, g], f"pass_{step}_{g}")
            dcp[step, g] = dcp[step, g] + [
                remote(
                    dbufs[step, g].at[pl.ds(4 * n, n)],
                    dbufs[step, g].at[pl.ds((4 + back(0, dy)) * n, n)],
                    ds.at[e, 4 + i],
                    dr.at[e, 4 + i],
                    plane_dev(0, dy),
                )
                for i, (_, dy) in enumerate(ROW)
            ]

    def stage_grad(step, g, finish):
        with jax.named_scope(f"wait_delta_{step}_{g}"):
            arrive(dcp[step, g], f"delta_{step}_{g}")
        with jax.named_scope(f"grad_{step}_{g}"):
            d = dbufs[step, g][...]
            for t in range(ROWS // TILE):
                rows = pl.ds(t * TILE, TILE)
                acc = lax.dot_general(
                    xbufs[step, g][:, rows], d, (((0,), (0,)), ((), ())), preferred_element_type=jnp.float32
                )
                if g > 0:
                    acc = acc + grad[rows]
                if finish is None:
                    grad[rows] = acc
                else:
                    finish(rows, acc * token_scale)

    def adamw(rows, g):
        m = beta_first * m_now[rows] + (1.0 - beta_first) * g
        v = beta_second * v_now[rows] + (1.0 - beta_second) * g * g
        w = w_now[rows].astype(jnp.float32)
        w = w - inner_rate * (m / (jnp.sqrt(v) + adam_eps) + decay_rate * w)
        return w.astype(jnp.bfloat16), m, v

    def finish_first(rows, g):
        w, m, v = adamw(rows, g)
        w_now[rows] = w
        m_now[rows] = m
        v_now[rows] = v

    def finish_last(rows, g):
        w, _, _ = adamw(rows, g)
        mixed = newanchor[rows]
        for k in range(KV):
            cols = slice(k * HEAD, (k + 1) * HEAD)
            mine = w[:, cols].astype(jnp.float32)
            chosen = lane_first > 0.5 if k == 0 else lane_first < 0.5
            out_w[0, rows, cols] = jnp.where(
                chosen, mix_local * mine + (1.0 - mix_local) * mixed, mine
            ).astype(jnp.bfloat16)

    def layer_sum(layer_cps):
        with jax.named_scope("layer_sum"):
            arrive(layer_cps, "layer")
            s = frag[segment(0, 0)].astype(jnp.float32)
            for i in range(len(LAYER)):
                s = s + layer_in[i].astype(jnp.float32)
            partial[...] = s
            cps = []
            for i, dh in enumerate(LAYERS):
                where = pl.ds(pl.multiple_of(lax.rem(zh + dh, 4) * PIECE, 8), PIECE)
                cps.append(remote(partial.at[where], pieces.at[i], ps.at[i], pr.at[i], stack_dev(dh)))
            return cps

    def stack_sum(cps):
        with jax.named_scope("stack_sum"):
            arrive(cps, "stack_sum")
            s = partial[pl.ds(pl.multiple_of(zh * PIECE, 8), PIECE)]
            for i in range(len(LAYERS)):
                s = s + pieces[i]
            mine = pl.ds(pl.multiple_of(layer_index(0, 0) * SEG + zh * PIECE, 8), PIECE)
            total[mine] = s
            out = []
            for i, dh in enumerate(LAYERS):
                out.append(remote(total.at[mine], total.at[mine], qs.at[i], qr.at[i], stack_dev(dh)))
            return out

    def layer_gather(cps):
        with jax.named_scope("layer_gather"):
            arrive(cps, "layer_gather")
            out = []
            for i, (dx, dc) in enumerate(LAYER):
                out.append(
                    remote(
                        total.at[segment(0, 0)], total.at[segment(0, 0)], ts.at[i], tr.at[i], layer_dev(dx, dc)
                    )
                )
            return out

    def outer(cps):
        with jax.named_scope("outer"):
            arrive(cps, "outer")
            get_anchor.wait()
            get_mom.wait()
            a = anchor[...]
            mean = a - total[...] * (1.0 / REPLICAS)
            nm = outer_beta * mom[...] + mean
            newmom[...] = nm
            newanchor[...] = a - outer_rate * (mean + outer_beta * nm)

    held = {}

    def act(kind, step, g):
        if kind == "raw":
            stage_raw(step, g)
        elif kind == "fold":
            stage_fold(step, g)
        elif kind == "delta":
            stage_delta(step, g)
        elif kind == "pass":
            stage_pass(step, g)
        elif kind == "grad":
            final = g == len(GROUPS[step]) - 1
            if final and step == 0:
                get_m.wait()
                get_v.wait()
            stage_grad(step, g, (finish_first, finish_last)[step] if final else None)
        elif kind == "scatter":
            held["sent"] = layer_scatter()
        elif kind == "layer":
            held["sent"] = layer_sum(held["sent"])
        elif kind == "stack":
            held["sent"] = stack_sum(held["sent"])
        elif kind == "gather":
            held["sent"] = layer_gather(held["sent"])
        elif kind == "outer":
            outer(held["sent"])

    open_layers()
    get_cot.wait()
    for k in range(len(UNITS)):
        landed(k)
        before = position
        position += UNITS[k][2]
        for mark, *what in PLAN:
            if before < mark <= position:
                act(*what)
        top_up()
    with jax.named_scope("write"):
        for cp in sends:
            cp.wait_send()


def flush(a_ref, b_ref, c_ref, a_out, b_out, c_out, sems):
    cps = []
    n = ROWS // PARTS
    for k in range(PARTS):
        part = pl.ds(k * n, n)
        cps.append(pltpu.make_async_copy(a_ref.at[0, part], a_out.at[0, part], sems.at[0, k]))
        cps.append(pltpu.make_async_copy(b_ref.at[part], b_out.at[part], sems.at[1, k]))
        cps.append(pltpu.make_async_copy(c_ref.at[part], c_out.at[part], sems.at[2, k]))
    for cp in cps:
        cp.start()
    for cp in cps:
        cp.wait()


def body(layer_input, cotangent, weight, first_moment, second_moment, key_gain, frag_index, anchor, momentum):
    bf, f32 = jnp.bfloat16, jnp.float32
    dma = pltpu.SemaphoreType.DMA
    any_spec = pl.BlockSpec(memory_space=pltpu.HBM)
    sizes = [GROUPS[s][g] for s, g in EXCH]
    scratch = [pltpu.VMEM((FSDP * n, ROWS), bf) for n in sizes]
    scratch += [pltpu.VMEM((FSDP * n, C), bf) for n in sizes]
    for e, n in zip(EXCH, sizes):
        shape = (3, n, C) if e in STAGED else (3, 2 * n, C) if e in YFIRST else (7, n, C)
        scratch.append(pltpu.VMEM(shape, bf))
    scratch += [pltpu.VMEM((FSDP * n, C), bf) for n in sizes]
    scratch += [pltpu.VMEM((4 * GROUPS[s][g], C), bf) for s, g in STAGED]
    scratch += [pltpu.VMEM((GROUPS[s][g], C), bf) for s, g in YFIRST]
    scratch += [pltpu.VMEM((4 * GROUPS[s][g], C), bf) for s, g in STAGED]
    scratch += [pltpu.VMEM((2 * GROUPS[s][g], C), bf) for s, g in YFIRST]
    scratch += [
        pltpu.VMEM((STEPS, TOK, C), bf),
        pltpu.VMEM((ROWS, C), bf),
        pltpu.VMEM((ROWS, C), f32),
        pltpu.VMEM((ROWS, C), f32),
        pltpu.VMEM((ROWS, C), f32),
        pltpu.VMEM((ROWS, HEAD), f32),
        pltpu.VMEM((ROWS, HEAD), f32),
        pltpu.VMEM((ROWS, HEAD), bf),
        pltpu.VMEM((len(LAYER), SEG, HEAD), bf),
        pltpu.VMEM((SEG, HEAD), f32),
        pltpu.VMEM((len(LAYERS), PIECE, HEAD), f32),
        pltpu.VMEM((ROWS, HEAD), f32),
        dma((6,)),
        dma((len(UNITS),)),
        dma((len(UNITS), 7)),
        dma((len(UNITS), 7)),
        dma((len(EXCH), 7)),
        dma((len(EXCH), 7)),
        dma((len(EXCH), 7)),
        dma((len(EXCH), 7)),
        dma((7,)),
        dma((7,)),
        dma((3,)),
        dma((3,)),
        dma((3,)),
        dma((3,)),
        dma((7,)),
        dma((7,)),
        dma((len(EXCH),)),
        dma((len(EXCH),)),
        pltpu.SemaphoreType.REGULAR,
    ]
    vmem_spec = pl.BlockSpec(memory_space=pltpu.VMEM)
    outs = pl.pallas_call(
        kernel,
        name="inner_outer",
        out_shape=(
            pltpu.VMEM((1, ROWS, C), bf),
            pltpu.VMEM((ROWS, HEAD), f32),
            pltpu.VMEM((ROWS, HEAD), f32),
        ),
        in_specs=[any_spec] * 5 + [vmem_spec, pl.BlockSpec(memory_space=pltpu.SMEM)] + [any_spec] * 2,
        out_specs=(vmem_spec, vmem_spec, vmem_spec),
        scratch_shapes=scratch,
        compiler_params=pltpu.CompilerParams(
            collective_id=0, has_side_effects=True, vmem_limit_bytes=LIMIT
        ),
    )(
        layer_input, cotangent, weight, first_moment, second_moment,
        key_gain.reshape(1, HEAD), frag_index, anchor, momentum,
    )
    outs = [pltpu.with_memory_space_constraint(o, pltpu.VMEM) for o in outs]
    return pl.pallas_call(
        flush,
        name="flush",
        out_shape=[jax.ShapeDtypeStruct(o.shape, o.dtype) for o in outs],
        in_specs=[vmem_spec] * 3,
        out_specs=[any_spec] * 3,
        scratch_shapes=[dma((3, PARTS))],
        compiler_params=pltpu.CompilerParams(vmem_limit_bytes=1 << 20),
    )(*outs)


def solution(mesh):
    placed = (
        P("replica", None, "fsdp", None),
        P("replica", None, "fsdp", None),
        P("replica", "fsdp", None),
        P("replica", "fsdp", None),
        P("replica", "fsdp", None),
        P(),
        P(),
        P("fsdp", None),
        P("fsdp", None),
    )
    return jax.shard_map(
        body,
        mesh=mesh,
        in_specs=placed,
        out_specs=(P("replica", "fsdp", None), P("fsdp", None), P("fsdp", None)),
        check_vma=False,
    )
```

```python
import math

import jax
import jax.numpy as jnp
from jax import lax
from jax.experimental import pallas as pl
from jax.experimental.pallas import tpu as pltpu
from jax.sharding import PartitionSpec as P

D = 12288
HEAD = 128
KV = 2
C = KV * HEAD
TOK = 128
STEPS = 2
FSDP = 8
ROWS = D // FSDP
REPLICAS = 32
GROUPS = ((80, 48), (64, 48, 16))
STAGED = ()
YFIRST = ((0, 0),)
PASSED = ((0, 0),)
ROW = ((0, 1), (0, 3), (0, 2))
PLAN = (
    (48, "scatter", 0, 0),
    (80, "raw", 0, 0),
    (112, "layer", 0, 0),
    (112, "fold", 0, 0),
    (128, "delta", 0, 0),
    (128, "raw", 0, 1),
    (144, "stack", 0, 0),
    (160, "pass", 0, 0),
    (160, "delta", 0, 1),
    (176, "gather", 0, 0),
    (176, "grad", 0, 0),
    (192, "grad", 0, 1),
    (192, "raw", 1, 0),
    (208, "outer", 0, 0),
    (240, "delta", 1, 0),
    (240, "raw", 1, 1),
    (256, "raw", 1, 2),
    (256, "delta", 1, 1),
    (256, "grad", 1, 0),
    (256, "delta", 1, 2),
    (256, "grad", 1, 1),
    (256, "grad", 1, 2),
)
SIZES = ((16,) * 8, (16,) * 8)
AHEAD = 48
UNITS = tuple((s, sum(SIZES[s][:i]), n) for s in range(STEPS) for i, n in enumerate(SIZES[s]))
EXCH = tuple((s, g) for s in range(STEPS) for g in range(len(GROUPS[s])))
TILE = 256
LIMIT = 54 << 20

beta_first = 0.9
beta_second = 0.95
inner_rate = 2.0
decay_rate = 0.05
adam_eps = 1e-08
norm_eps = 1e-06
outer_rate = 0.7
outer_beta = 0.9
mix_local = 0.5

PLANE = ((1, 2), (0, 2), (1, 1), (1, 3), (0, 1), (0, 3), (1, 0))
LAYER = tuple((dx, dc) for dx in (2, 1, 3, 0) for dc in (0, 1) if (dx, dc) != (0, 0))
LAYERS = (2, 1, 3)
SEG = ROWS // 8
PIECE = SEG // 4
MESH = pl.DeviceIdType.MESH


def kernel(
    x_hbm, cot_hbm, w_hbm, m_hbm, v_hbm, gain_ref, frag_ref, anchor_hbm, mom_hbm,
    w_now, m_now, v_now, grad, newmom, newanchor,
    *scratch,
):
    count = len(EXCH)
    xbufs = dict(zip(EXCH, scratch[:count]))
    rsends = dict(zip(EXCH, scratch[count : 2 * count]))
    rrecvs = dict(zip(EXCH, scratch[2 * count : 3 * count]))
    dbufs = dict(zip(EXCH, scratch[3 * count : 4 * count]))
    both = STAGED + YFIRST
    split = 4 * count + len(both)
    zrecvs = dict(zip(both, scratch[4 * count : split]))
    folds = dict(zip(both, scratch[split : split + len(both)]))
    (
        cot, anchor, mom, frag, layer_in, partial, pieces, total,
        loc_sem, own_sem, xs, xr, rs, rr, ds, dr, ls, lr, ps, pr, qs, qr, ts, tr, zs, zr, go_sem,
    ) = scratch[split + len(both) :]
    rep = lax.axis_index("replica")
    fs = lax.axis_index("fsdp")
    zl, yy = fs // 4, lax.rem(fs, 4)
    zh, xx, cc = rep // 8, lax.rem(rep // 2, 4), lax.rem(rep, 2)

    def plane_index(dz, dy):
        return lax.rem(zl + dz, 2) * 4 + lax.rem(yy + dy, 4)

    def layer_index(dx, dc):
        return lax.rem(xx + dx, 4) * 2 + lax.rem(cc + dc, 2)

    def plane_dev(dz, dy):
        return (rep, plane_index(dz, dy))

    def layer_dev(dx, dc):
        return (zh * 8 + layer_index(dx, dc), fs)

    def stack_dev(dh):
        return (lax.rem(zh + dh, 4) * 8 + xx * 2 + cc, fs)

    leader = rep == REPLICAS - 1
    with jax.named_scope("entry"):
        bar = pltpu.get_barrier_semaphore()
        for o in PLANE:
            pl.semaphore_signal(bar, inc=1, device_id=plane_dev(*o), device_id_type=MESH)

        @pl.when(jnp.logical_not(leader))
        def _():
            pl.semaphore_signal(bar, inc=1, device_id=(REPLICAS - 1, fs), device_id_type=MESH)
            pl.semaphore_wait(bar, len(PLANE))

        @pl.when(leader)
        def _():
            pl.semaphore_wait(bar, len(PLANE) + REPLICAS - 1)

    sends = []

    def remote(src, dst, s, r, dev):
        cp = pltpu.make_async_remote_copy(
            src_ref=src, dst_ref=dst, send_sem=s, recv_sem=r, device_id=dev, device_id_type=MESH
        )
        cp.start()
        sends.append(cp)
        return cp

    def arrive(cps, name):
        for cp in cps:
            cp.wait_recv()

    def slot(dz, dy):
        return dz * 4 + dy

    def back(dz, dy):
        return dz * 4 + (4 - dy) % 4

    def columns(dz, dy):
        return pl.ds(pl.multiple_of(plane_index(dz, dy) * ROWS, 128), ROWS)

    def place(step, row):
        g = 0
        while row >= GROUPS[step][g]:
            row -= GROUPS[step][g]
            g += 1
        return g, row

    def send_x(k):
        step, row, rows = UNITS[k]
        g, at = place(step, row)
        n = GROUPS[step][g]
        got = []
        for i, o in enumerate(PLANE):
            got.append(
                remote(
                    x_hbm.at[0, step, pl.ds(row, rows), columns(*o)],
                    xbufs[step, g].at[pl.ds(back(*o) * n + at, rows)],
                    xs.at[k, i],
                    xr.at[k, i],
                    plane_dev(*o),
                )
            )
        own = pltpu.make_async_copy(
            x_hbm.at[0, step, pl.ds(row, rows), columns(0, 0)],
            xbufs[step, g].at[pl.ds(at, rows)],
            own_sem.at[k],
        )
        own.start()
        return got, own

    def local(src, dst, i):
        cp = pltpu.make_async_copy(src, dst, loc_sem.at[i])
        cp.start()
        return cp

    xcp = {}

    def issue(k):
        if k < len(UNITS):
            with jax.named_scope("send_x"):
                xcp[k] = send_x(k)

    def landed(k):
        with jax.named_scope("wait_x"):
            got, own = xcp[k]
            own.wait()
            arrive(got, f"x_{k}")

    issued = 0
    done = 0
    position = 0

    def top_up():
        nonlocal issued, done
        while issued < len(UNITS) and (issued == 0 or sum(u[2] for u in UNITS[:issued]) < position + AHEAD):
            issue(issued)
            issued += 1

    top_up()
    get_w = local(w_hbm.at[0], w_now, 0)
    get_cot = local(cot_hbm.at[0], cot, 1)
    get_m = local(m_hbm.at[0], m_now, 2)
    get_v = local(v_hbm.at[0], v_now, 3)
    get_anchor = local(anchor_hbm, anchor, 4)
    get_mom = local(mom_hbm, mom, 5)

    first_frag = lax.rem(frag_ref[0], KV) == 0
    lane_first = jnp.where(first_frag, jnp.float32(1.0), jnp.float32(0.0))

    def segment(dx, dc):
        return pl.ds(pl.multiple_of(layer_index(dx, dc) * SEG, 16), SEG)

    def open_layers():
        with jax.named_scope("open_layers"):

            @pl.when(leader)
            def _():
                @pl.loop(0, REPLICAS - 1)
                def _(r):
                    pl.semaphore_signal(go_sem, inc=1, device_id=(r, fs), device_id_type=MESH)

            get_w.wait()
            frag[...] = jnp.where(
                lane_first > 0.5, w_now[:, :HEAD].astype(jnp.float32), w_now[:, HEAD:].astype(jnp.float32)
            ).astype(jnp.bfloat16)

    def layer_scatter():
        with jax.named_scope("layer_scatter"):

            @pl.when(jnp.logical_not(leader))
            def _():
                pl.semaphore_wait(go_sem, 1)

            return [
                remote(frag.at[segment(dx, dc)], layer_in.at[i], ls.at[i], lr.at[i], layer_dev(dx, dc))
                for i, (dx, dc) in enumerate(LAYER)
            ]

    width_scale = 1.0 / math.sqrt(D)
    token_scale = 1.0 / math.sqrt(TOK * FSDP)
    rcp, dcp = {}, {}
    mcp, zcp, fcp = {}, {}, {}

    def stage_raw(step, g):
        n = GROUPS[step][g]
        e = EXCH.index((step, g))
        with jax.named_scope(f"raw_{step}_{g}"):
            rsends[step, g][...] = jnp.dot(
                xbufs[step, g][...], w_now[...], preferred_element_type=jnp.float32
            ).astype(jnp.bfloat16)
            if (step, g) in STAGED:
                mcp[step, g] = [
                    remote(
                        rsends[step, g].at[pl.ds(4 * n, 4 * n)],
                        zrecvs[step, g],
                        zs.at[e],
                        zr.at[e],
                        plane_dev(1, 0),
                    )
                ]
                return
            if (step, g) in YFIRST:
                mcp[step, g] = [
                    remote(
                        rsends[step, g].at[pl.ds((4 * half + dy) * n, n)],
                        rrecvs[step, g].at[i, pl.ds(half * n, n)],
                        rs.at[e, 2 * i + half],
                        rr.at[e, 2 * i + half],
                        plane_dev(0, dy),
                    )
                    for i, (_, dy) in enumerate(ROW)
                    for half in range(2)
                ]
                return
            rcp[step, g] = [
                remote(
                    rsends[step, g].at[pl.ds(slot(*o) * n, n)],
                    rrecvs[step, g].at[i],
                    rs.at[e, i],
                    rr.at[e, i],
                    plane_dev(*o),
                )
                for i, o in enumerate(PLANE)
            ]

    def stage_fold(step, g):
        n = GROUPS[step][g]
        e = EXCH.index((step, g))
        with jax.named_scope(f"fold_{step}_{g}"):
            arrive(mcp[step, g], f"fold_{step}_{g}")
            if (step, g) in YFIRST:
                for half in range(2):
                    total_half = rsends[step, g][4 * half * n : (4 * half + 1) * n].astype(jnp.float32)
                    for i in range(len(ROW)):
                        total_half = total_half + rrecvs[step, g][i, half * n : (half + 1) * n].astype(jnp.float32)
                    folds[step, g][half * n : (half + 1) * n] = total_half.astype(jnp.bfloat16)
                rcp[step, g] = [
                    remote(
                        folds[step, g].at[pl.ds(n, n)], zrecvs[step, g], zs.at[e], zr.at[e], plane_dev(1, 0)
                    )
                ]
                return
            folds[step, g][...] = (
                rsends[step, g][: 4 * n].astype(jnp.float32) + zrecvs[step, g][...].astype(jnp.float32)
            ).astype(jnp.bfloat16)
            rcp[step, g] = [
                remote(
                    folds[step, g].at[pl.ds(dy * n, n)],
                    rrecvs[step, g].at[i],
                    rs.at[e, i],
                    rr.at[e, i],
                    plane_dev(0, dy),
                )
                for i, (_, dy) in enumerate(ROW)
            ]

    def stage_delta(step, g):
        n = GROUPS[step][g]
        e = EXCH.index((step, g))
        staged = (step, g) in STAGED
        yfirst = (step, g) in YFIRST
        passed = (step, g) in PASSED
        with jax.named_scope(f"wait_raw_{step}_{g}"):
            arrive(rcp[step, g], f"raw_{step}_{g}")
        with jax.named_scope(f"delta_{step}_{g}"):
            mine = folds[step, g] if staged or yfirst else rsends[step, g]
            raw = mine[:n].astype(jnp.float32)
            if yfirst:
                raw = raw + zrecvs[step, g][...].astype(jnp.float32)
            else:
                for i in range(len(rcp[step, g])):
                    raw = raw + rrecvs[step, g][i].astype(jnp.float32)
            raw = raw * width_scale
            up = cot[step, pl.ds(sum(GROUPS[step][:g]), n)].astype(jnp.float32)
            gain = gain_ref[...]
            for k in range(KV):
                cols = slice(k * HEAD, (k + 1) * HEAD)
                r = raw[:, cols]
                p = up[:, cols] * gain
                inv = lax.rsqrt(jnp.mean(r * r, axis=-1, keepdims=True) + norm_eps)
                dotp = jnp.mean(p * r, axis=-1, keepdims=True)
                dbufs[step, g][:n, cols] = (inv * p - r * (inv * inv * inv) * dotp).astype(jnp.bfloat16)
            targets = ((1, 0),) + ROW if passed else PLANE
            cps = [
                remote(
                    dbufs[step, g].at[pl.ds(0, n)],
                    dbufs[step, g].at[pl.ds(back(*o) * n, n)],
                    ds.at[e, i],
                    dr.at[e, i],
                    plane_dev(*o),
                )
                for i, o in enumerate(targets)
            ]
            if passed:
                zcp[step, g], cps = cps[:1], cps[1:]
            dcp[step, g] = cps

    def stage_pass(step, g):
        n = GROUPS[step][g]
        e = EXCH.index((step, g))
        with jax.named_scope(f"pass_{step}_{g}"):
            arrive(zcp[step, g], f"pass_{step}_{g}")
            dcp[step, g] = dcp[step, g] + [
                remote(
                    dbufs[step, g].at[pl.ds(4 * n, n)],
                    dbufs[step, g].at[pl.ds((4 + back(0, dy)) * n, n)],
                    ds.at[e, 4 + i],
                    dr.at[e, 4 + i],
                    plane_dev(0, dy),
                )
                for i, (_, dy) in enumerate(ROW)
            ]

    def stage_grad(step, g, finish):
        with jax.named_scope(f"wait_delta_{step}_{g}"):
            arrive(dcp[step, g], f"delta_{step}_{g}")
        with jax.named_scope(f"grad_{step}_{g}"):
            d = dbufs[step, g][...]
            for t in range(ROWS // TILE):
                rows = pl.ds(t * TILE, TILE)
                acc = lax.dot_general(
                    xbufs[step, g][:, rows], d, (((0,), (0,)), ((), ())), preferred_element_type=jnp.float32
                )
                if g > 0:
                    acc = acc + grad[rows]
                if finish is None:
                    grad[rows] = acc
                else:
                    finish(rows, acc * token_scale)

    def finish_first(rows, g):
        w, m, v = adamw(w_now[rows], m_now[rows], v_now[rows], g)
        w_now[rows] = w
        m_now[rows] = m
        v_now[rows] = v

    def finish_last(rows, g):
        grad[rows] = g

    def layer_sum(layer_cps):
        with jax.named_scope("layer_sum"):
            arrive(layer_cps, "layer")
            s = frag[segment(0, 0)].astype(jnp.float32)
            for i in range(len(LAYER)):
                s = s + layer_in[i].astype(jnp.float32)
            partial[...] = s
            cps = []
            for i, dh in enumerate(LAYERS):
                where = pl.ds(pl.multiple_of(lax.rem(zh + dh, 4) * PIECE, 8), PIECE)
                cps.append(remote(partial.at[where], pieces.at[i], ps.at[i], pr.at[i], stack_dev(dh)))
            return cps

    def stack_sum(cps):
        with jax.named_scope("stack_sum"):
            arrive(cps, "stack_sum")
            s = partial[pl.ds(pl.multiple_of(zh * PIECE, 8), PIECE)]
            for i in range(len(LAYERS)):
                s = s + pieces[i]
            mine = pl.ds(pl.multiple_of(layer_index(0, 0) * SEG + zh * PIECE, 8), PIECE)
            total[mine] = s
            out = []
            for i, dh in enumerate(LAYERS):
                out.append(remote(total.at[mine], total.at[mine], qs.at[i], qr.at[i], stack_dev(dh)))
            return out

    def layer_gather(cps):
        with jax.named_scope("layer_gather"):
            arrive(cps, "layer_gather")
            out = []
            for i, (dx, dc) in enumerate(LAYER):
                out.append(
                    remote(
                        total.at[segment(0, 0)], total.at[segment(0, 0)], ts.at[i], tr.at[i], layer_dev(dx, dc)
                    )
                )
            return out

    def outer(cps):
        with jax.named_scope("outer"):
            arrive(cps, "outer")
            get_anchor.wait()
            get_mom.wait()
            a = anchor[...]
            mean = a - total[...] * (1.0 / REPLICAS)
            nm = outer_beta * mom[...] + mean
            newmom[...] = nm
            newanchor[...] = a - outer_rate * (mean + outer_beta * nm)

    held = {}

    def act(kind, step, g):
        if kind == "raw":
            stage_raw(step, g)
        elif kind == "fold":
            stage_fold(step, g)
        elif kind == "delta":
            stage_delta(step, g)
        elif kind == "pass":
            stage_pass(step, g)
        elif kind == "grad":
            final = g == len(GROUPS[step]) - 1
            if final and step == 0:
                get_m.wait()
                get_v.wait()
            stage_grad(step, g, (finish_first, finish_last)[step] if final else None)
        elif kind == "scatter":
            held["sent"] = layer_scatter()
        elif kind == "layer":
            held["sent"] = layer_sum(held["sent"])
        elif kind == "stack":
            held["sent"] = stack_sum(held["sent"])
        elif kind == "gather":
            held["sent"] = layer_gather(held["sent"])
        elif kind == "outer":
            outer(held["sent"])

    open_layers()
    get_cot.wait()
    for k in range(len(UNITS)):
        landed(k)
        before = position
        position += UNITS[k][2]
        for mark, *what in PLAN:
            if before < mark <= position:
                act(*what)
        top_up()
    with jax.named_scope("write"):
        for cp in sends:
            cp.wait_send()


def adamw(w, m, v, g):
    m = beta_first * m + (1.0 - beta_first) * g
    v = beta_second * v + (1.0 - beta_second) * g * g
    w = w.astype(jnp.float32)
    w = w - inner_rate * (m / (jnp.sqrt(v) + adam_eps) + decay_rate * w)
    return w.astype(jnp.bfloat16), m, v


def finish(
    frag_ref, w_ref, m_ref, v_ref, g_ref, mom_ref, anchor_ref,
    merged_out, mom_out, anchor_out, merged, sems, tile_sems,
):
    cps = [
        pltpu.make_async_copy(mom_ref, mom_out, sems.at[0]),
        pltpu.make_async_copy(anchor_ref, anchor_out, sems.at[1]),
    ]
    for cp in cps:
        cp.start()
    first = lax.rem(frag_ref[0], KV) == 0
    lane_first = jnp.where(first, jnp.float32(1.0), jnp.float32(0.0))
    for t in range(ROWS // TILE):
        rows = pl.ds(t * TILE, TILE)
        w, _, _ = adamw(w_ref[rows], m_ref[rows], v_ref[rows], g_ref[rows])
        mixed = anchor_ref[rows]
        for k in range(KV):
            cols = slice(k * HEAD, (k + 1) * HEAD)
            mine = w[:, cols].astype(jnp.float32)
            chosen = lane_first > 0.5 if k == 0 else lane_first < 0.5
            merged[rows, cols] = jnp.where(
                chosen, mix_local * mine + (1.0 - mix_local) * mixed, mine
            ).astype(jnp.bfloat16)
        cp = pltpu.make_async_copy(merged.at[rows], merged_out.at[0, rows], tile_sems.at[t])
        cp.start()
        cps.append(cp)
    for cp in cps:
        cp.wait()


def body(layer_input, cotangent, weight, first_moment, second_moment, key_gain, frag_index, anchor, momentum):
    bf, f32 = jnp.bfloat16, jnp.float32
    dma = pltpu.SemaphoreType.DMA
    any_spec = pl.BlockSpec(memory_space=pltpu.HBM)
    sizes = [GROUPS[s][g] for s, g in EXCH]
    scratch = [pltpu.VMEM((FSDP * n, ROWS), bf) for n in sizes]
    scratch += [pltpu.VMEM((FSDP * n, C), bf) for n in sizes]
    for e, n in zip(EXCH, sizes):
        shape = (3, n, C) if e in STAGED else (3, 2 * n, C) if e in YFIRST else (7, n, C)
        scratch.append(pltpu.VMEM(shape, bf))
    scratch += [pltpu.VMEM((FSDP * n, C), bf) for n in sizes]
    scratch += [pltpu.VMEM((4 * GROUPS[s][g], C), bf) for s, g in STAGED]
    scratch += [pltpu.VMEM((GROUPS[s][g], C), bf) for s, g in YFIRST]
    scratch += [pltpu.VMEM((4 * GROUPS[s][g], C), bf) for s, g in STAGED]
    scratch += [pltpu.VMEM((2 * GROUPS[s][g], C), bf) for s, g in YFIRST]
    scratch += [
        pltpu.VMEM((STEPS, TOK, C), bf),
        pltpu.VMEM((ROWS, HEAD), f32),
        pltpu.VMEM((ROWS, HEAD), f32),
        pltpu.VMEM((ROWS, HEAD), bf),
        pltpu.VMEM((len(LAYER), SEG, HEAD), bf),
        pltpu.VMEM((SEG, HEAD), f32),
        pltpu.VMEM((len(LAYERS), PIECE, HEAD), f32),
        pltpu.VMEM((ROWS, HEAD), f32),
        dma((6,)),
        dma((len(UNITS),)),
        dma((len(UNITS), 7)),
        dma((len(UNITS), 7)),
        dma((len(EXCH), 7)),
        dma((len(EXCH), 7)),
        dma((len(EXCH), 7)),
        dma((len(EXCH), 7)),
        dma((7,)),
        dma((7,)),
        dma((3,)),
        dma((3,)),
        dma((3,)),
        dma((3,)),
        dma((7,)),
        dma((7,)),
        dma((len(EXCH),)),
        dma((len(EXCH),)),
        pltpu.SemaphoreType.REGULAR,
    ]
    vmem_spec = pl.BlockSpec(memory_space=pltpu.VMEM)
    outs = pl.pallas_call(
        kernel,
        name="inner_outer",
        out_shape=(
            pltpu.VMEM((ROWS, C), bf),
            pltpu.VMEM((ROWS, C), f32),
            pltpu.VMEM((ROWS, C), f32),
            pltpu.VMEM((ROWS, C), f32),
            pltpu.VMEM((ROWS, HEAD), f32),
            pltpu.VMEM((ROWS, HEAD), f32),
        ),
        in_specs=[any_spec] * 5 + [vmem_spec, pl.BlockSpec(memory_space=pltpu.SMEM)] + [any_spec] * 2,
        out_specs=(vmem_spec,) * 6,
        scratch_shapes=scratch,
        compiler_params=pltpu.CompilerParams(
            collective_id=0, has_side_effects=True, vmem_limit_bytes=LIMIT
        ),
    )(
        layer_input, cotangent, weight, first_moment, second_moment,
        key_gain.reshape(1, HEAD), frag_index, anchor, momentum,
    )
    outs = [pltpu.with_memory_space_constraint(o, pltpu.VMEM) for o in outs]
    return pl.pallas_call(
        finish,
        name="finish",
        out_shape=[
            jax.ShapeDtypeStruct((1, ROWS, C), bf),
            jax.ShapeDtypeStruct((ROWS, HEAD), f32),
            jax.ShapeDtypeStruct((ROWS, HEAD), f32),
        ],
        in_specs=[pl.BlockSpec(memory_space=pltpu.SMEM)] + [vmem_spec] * 6,
        out_specs=[any_spec] * 3,
        scratch_shapes=[pltpu.VMEM((ROWS, C), bf), dma((2,)), dma((ROWS // TILE,))],
        compiler_params=pltpu.CompilerParams(vmem_limit_bytes=2 << 20),
    )(frag_index, *outs)


def solution(mesh):
    placed = (
        P("replica", None, "fsdp", None),
        P("replica", None, "fsdp", None),
        P("replica", "fsdp", None),
        P("replica", "fsdp", None),
        P("replica", "fsdp", None),
        P(),
        P(),
        P("fsdp", None),
        P("fsdp", None),
    )
    return jax.shard_map(
        body,
        mesh=mesh,
        in_specs=placed,
        out_specs=(P("replica", "fsdp", None), P("fsdp", None), P("fsdp", None)),
        check_vma=False,
    )
```

```python
import math

import jax
import jax.numpy as jnp
from jax import lax
from jax.experimental import pallas as pl
from jax.experimental.pallas import tpu as pltpu
from jax.sharding import PartitionSpec as P

D = 12288
HEAD = 128
KV = 2
C = KV * HEAD
TOK = 128
STEPS = 2
FSDP = 8
ROWS = D // FSDP
REPLICAS = 32
LEADER = 21
GROUPS = ((80, 48), (64, 48, 16))
STAGED = ()
YFIRST = ((0, 0),)
PASSED = ((0, 0),)
ROW = ((0, 1), (0, 3), (0, 2))
PLAN = (
    (48, "scatter", 0, 0),
    (80, "raw", 0, 0),
    (112, "layer", 0, 0),
    (112, "fold", 0, 0),
    (128, "delta", 0, 0),
    (128, "raw", 0, 1),
    (144, "stack", 0, 0),
    (160, "pass", 0, 0),
    (160, "delta", 0, 1),
    (176, "gather", 0, 0),
    (176, "grad", 0, 0),
    (192, "grad", 0, 1),
    (192, "raw", 1, 0),
    (208, "outer", 0, 0),
    (240, "delta", 1, 0),
    (240, "raw", 1, 1),
    (256, "raw", 1, 2),
    (256, "delta", 1, 1),
    (256, "grad", 1, 0),
    (256, "delta", 1, 2),
    (256, "grad", 1, 1),
    (256, "grad", 1, 2),
)
SIZES = ((16,) * 8, (16,) * 8)
AHEAD = 48
UNITS = tuple((s, sum(SIZES[s][:i]), n) for s in range(STEPS) for i, n in enumerate(SIZES[s]))
EXCH = tuple((s, g) for s in range(STEPS) for g in range(len(GROUPS[s])))
TILE = 256
LIMIT = 54 << 20

beta_first = 0.9
beta_second = 0.95
inner_rate = 2.0
decay_rate = 0.05
adam_eps = 1e-08
norm_eps = 1e-06
outer_rate = 0.7
outer_beta = 0.9
mix_local = 0.5

PLANE = ((1, 2), (0, 2), (1, 1), (1, 3), (0, 1), (0, 3), (1, 0))
LAYER = tuple((dx, dc) for dx in (2, 1, 3, 0) for dc in (0, 1) if (dx, dc) != (0, 0))
LAYERS = (2, 1, 3)
SEG = ROWS // 8
PIECE = SEG // 4
MESH = pl.DeviceIdType.MESH


def kernel(
    x_hbm, cot_hbm, w_hbm, m_hbm, v_hbm, gain_ref, frag_ref, anchor_hbm, mom_hbm,
    w_now, m_now, v_now, grad, newmom, newanchor,
    *scratch,
):
    count = len(EXCH)
    xbufs = dict(zip(EXCH, scratch[:count]))
    rsends = dict(zip(EXCH, scratch[count : 2 * count]))
    rrecvs = dict(zip(EXCH, scratch[2 * count : 3 * count]))
    dbufs = dict(zip(EXCH, scratch[3 * count : 4 * count]))
    both = STAGED + YFIRST
    split = 4 * count + len(both)
    zrecvs = dict(zip(both, scratch[4 * count : split]))
    folds = dict(zip(both, scratch[split : split + len(both)]))
    (
        cot, anchor, mom, frag, layer_in, partial, pieces, total,
        loc_sem, own_sem, xs, xr, rs, rr, ds, dr, ls, lr, ps, pr, qs, qr, ts, tr, zs, zr, go_sem,
    ) = scratch[split + len(both) :]
    rep = lax.axis_index("replica")
    fs = lax.axis_index("fsdp")
    zl, yy = fs // 4, lax.rem(fs, 4)
    zh, xx, cc = rep // 8, lax.rem(rep // 2, 4), lax.rem(rep, 2)

    def plane_index(dz, dy):
        return lax.rem(zl + dz, 2) * 4 + lax.rem(yy + dy, 4)

    def layer_index(dx, dc):
        return lax.rem(xx + dx, 4) * 2 + lax.rem(cc + dc, 2)

    def plane_dev(dz, dy):
        return (rep, plane_index(dz, dy))

    def layer_dev(dx, dc):
        return (zh * 8 + layer_index(dx, dc), fs)

    def stack_dev(dh):
        return (lax.rem(zh + dh, 4) * 8 + xx * 2 + cc, fs)

    leader = rep == LEADER
    with jax.named_scope("entry"):
        bar = pltpu.get_barrier_semaphore()
        for o in PLANE:
            pl.semaphore_signal(bar, inc=1, device_id=plane_dev(*o), device_id_type=MESH)

        @pl.when(jnp.logical_not(leader))
        def _():
            pl.semaphore_signal(bar, inc=1, device_id=(LEADER, fs), device_id_type=MESH)
            pl.semaphore_wait(bar, len(PLANE))

        @pl.when(leader)
        def _():
            pl.semaphore_wait(bar, len(PLANE) + REPLICAS - 1)

    sends = []

    def remote(src, dst, s, r, dev):
        cp = pltpu.make_async_remote_copy(
            src_ref=src, dst_ref=dst, send_sem=s, recv_sem=r, device_id=dev, device_id_type=MESH
        )
        cp.start()
        sends.append(cp)
        return cp

    def arrive(cps, name):
        for cp in cps:
            cp.wait_recv()

    def slot(dz, dy):
        return dz * 4 + dy

    def back(dz, dy):
        return dz * 4 + (4 - dy) % 4

    def columns(dz, dy):
        return pl.ds(pl.multiple_of(plane_index(dz, dy) * ROWS, 128), ROWS)

    def place(step, row):
        g = 0
        while row >= GROUPS[step][g]:
            row -= GROUPS[step][g]
            g += 1
        return g, row

    def send_x(k):
        step, row, rows = UNITS[k]
        g, at = place(step, row)
        n = GROUPS[step][g]
        got = []
        for i, o in enumerate(PLANE):
            got.append(
                remote(
                    x_hbm.at[0, step, pl.ds(row, rows), columns(*o)],
                    xbufs[step, g].at[pl.ds(back(*o) * n + at, rows)],
                    xs.at[k, i],
                    xr.at[k, i],
                    plane_dev(*o),
                )
            )
        own = pltpu.make_async_copy(
            x_hbm.at[0, step, pl.ds(row, rows), columns(0, 0)],
            xbufs[step, g].at[pl.ds(at, rows)],
            own_sem.at[k],
        )
        own.start()
        return got, own

    def local(src, dst, i):
        cp = pltpu.make_async_copy(src, dst, loc_sem.at[i])
        cp.start()
        return cp

    xcp = {}

    def issue(k):
        if k < len(UNITS):
            with jax.named_scope("send_x"):
                xcp[k] = send_x(k)

    def landed(k):
        with jax.named_scope("wait_x"):
            got, own = xcp[k]
            own.wait()
            arrive(got, f"x_{k}")

    issued = 0
    done = 0
    position = 0

    def top_up():
        nonlocal issued, done
        while issued < len(UNITS) and (issued == 0 or sum(u[2] for u in UNITS[:issued]) < position + AHEAD):
            issue(issued)
            issued += 1

    top_up()
    get_w = local(w_hbm.at[0], w_now, 0)
    get_cot = local(cot_hbm.at[0], cot, 1)
    get_m = local(m_hbm.at[0], m_now, 2)
    get_v = local(v_hbm.at[0], v_now, 3)
    get_anchor = local(anchor_hbm, anchor, 4)
    get_mom = local(mom_hbm, mom, 5)

    first_frag = lax.rem(frag_ref[0], KV) == 0
    lane_first = jnp.where(first_frag, jnp.float32(1.0), jnp.float32(0.0))

    def segment(dx, dc):
        return pl.ds(pl.multiple_of(layer_index(dx, dc) * SEG, 16), SEG)

    def open_layers():
        with jax.named_scope("open_layers"):

            @pl.when(leader)
            def _():
                @pl.loop(1, REPLICAS)
                def _(r):
                    pl.semaphore_signal(go_sem, inc=1, device_id=(lax.rem(LEADER + r, REPLICAS), fs), device_id_type=MESH)

            get_w.wait()
            frag[...] = jnp.where(
                lane_first > 0.5, w_now[:, :HEAD].astype(jnp.float32), w_now[:, HEAD:].astype(jnp.float32)
            ).astype(jnp.bfloat16)

    def layer_scatter():
        with jax.named_scope("layer_scatter"):

            @pl.when(jnp.logical_not(leader))
            def _():
                pl.semaphore_wait(go_sem, 1)

            return [
                remote(frag.at[segment(dx, dc)], layer_in.at[i], ls.at[i], lr.at[i], layer_dev(dx, dc))
                for i, (dx, dc) in enumerate(LAYER)
            ]

    width_scale = 1.0 / math.sqrt(D)
    token_scale = 1.0 / math.sqrt(TOK * FSDP)
    rcp, dcp = {}, {}
    mcp, zcp, fcp = {}, {}, {}

    def stage_raw(step, g):
        n = GROUPS[step][g]
        e = EXCH.index((step, g))
        with jax.named_scope(f"raw_{step}_{g}"):
            rsends[step, g][...] = jnp.dot(
                xbufs[step, g][...], w_now[...], preferred_element_type=jnp.float32
            ).astype(jnp.bfloat16)
            if (step, g) in STAGED:
                mcp[step, g] = [
                    remote(
                        rsends[step, g].at[pl.ds(4 * n, 4 * n)],
                        zrecvs[step, g],
                        zs.at[e],
                        zr.at[e],
                        plane_dev(1, 0),
                    )
                ]
                return
            if (step, g) in YFIRST:
                mcp[step, g] = [
                    remote(
                        rsends[step, g].at[pl.ds((4 * half + dy) * n, n)],
                        rrecvs[step, g].at[i, pl.ds(half * n, n)],
                        rs.at[e, 2 * i + half],
                        rr.at[e, 2 * i + half],
                        plane_dev(0, dy),
                    )
                    for i, (_, dy) in enumerate(ROW)
                    for half in range(2)
                ]
                return
            rcp[step, g] = [
                remote(
                    rsends[step, g].at[pl.ds(slot(*o) * n, n)],
                    rrecvs[step, g].at[i],
                    rs.at[e, i],
                    rr.at[e, i],
                    plane_dev(*o),
                )
                for i, o in enumerate(PLANE)
            ]

    def stage_fold(step, g):
        n = GROUPS[step][g]
        e = EXCH.index((step, g))
        with jax.named_scope(f"fold_{step}_{g}"):
            arrive(mcp[step, g], f"fold_{step}_{g}")
            if (step, g) in YFIRST:
                for half in range(2):
                    total_half = rsends[step, g][4 * half * n : (4 * half + 1) * n].astype(jnp.float32)
                    for i in range(len(ROW)):
                        total_half = total_half + rrecvs[step, g][i, half * n : (half + 1) * n].astype(jnp.float32)
                    folds[step, g][half * n : (half + 1) * n] = total_half.astype(jnp.bfloat16)
                rcp[step, g] = [
                    remote(
                        folds[step, g].at[pl.ds(n, n)], zrecvs[step, g], zs.at[e], zr.at[e], plane_dev(1, 0)
                    )
                ]
                return
            folds[step, g][...] = (
                rsends[step, g][: 4 * n].astype(jnp.float32) + zrecvs[step, g][...].astype(jnp.float32)
            ).astype(jnp.bfloat16)
            rcp[step, g] = [
                remote(
                    folds[step, g].at[pl.ds(dy * n, n)],
                    rrecvs[step, g].at[i],
                    rs.at[e, i],
                    rr.at[e, i],
                    plane_dev(0, dy),
                )
                for i, (_, dy) in enumerate(ROW)
            ]

    def stage_delta(step, g):
        n = GROUPS[step][g]
        e = EXCH.index((step, g))
        staged = (step, g) in STAGED
        yfirst = (step, g) in YFIRST
        passed = (step, g) in PASSED
        with jax.named_scope(f"wait_raw_{step}_{g}"):
            arrive(rcp[step, g], f"raw_{step}_{g}")
        with jax.named_scope(f"delta_{step}_{g}"):
            mine = folds[step, g] if staged or yfirst else rsends[step, g]
            raw = mine[:n].astype(jnp.float32)
            if yfirst:
                raw = raw + zrecvs[step, g][...].astype(jnp.float32)
            else:
                for i in range(len(rcp[step, g])):
                    raw = raw + rrecvs[step, g][i].astype(jnp.float32)
            raw = raw * width_scale
            up = cot[step, pl.ds(sum(GROUPS[step][:g]), n)].astype(jnp.float32)
            gain = gain_ref[...]
            for k in range(KV):
                cols = slice(k * HEAD, (k + 1) * HEAD)
                r = raw[:, cols]
                p = up[:, cols] * gain
                inv = lax.rsqrt(jnp.mean(r * r, axis=-1, keepdims=True) + norm_eps)
                dotp = jnp.mean(p * r, axis=-1, keepdims=True)
                dbufs[step, g][:n, cols] = (inv * p - r * (inv * inv * inv) * dotp).astype(jnp.bfloat16)
            targets = ((1, 0),) + ROW if passed else PLANE
            cps = [
                remote(
                    dbufs[step, g].at[pl.ds(0, n)],
                    dbufs[step, g].at[pl.ds(back(*o) * n, n)],
                    ds.at[e, i],
                    dr.at[e, i],
                    plane_dev(*o),
                )
                for i, o in enumerate(targets)
            ]
            if passed:
                zcp[step, g], cps = cps[:1], cps[1:]
            dcp[step, g] = cps

    def stage_pass(step, g):
        n = GROUPS[step][g]
        e = EXCH.index((step, g))
        with jax.named_scope(f"pass_{step}_{g}"):
            arrive(zcp[step, g], f"pass_{step}_{g}")
            dcp[step, g] = dcp[step, g] + [
                remote(
                    dbufs[step, g].at[pl.ds(4 * n, n)],
                    dbufs[step, g].at[pl.ds((4 + back(0, dy)) * n, n)],
                    ds.at[e, 4 + i],
                    dr.at[e, 4 + i],
                    plane_dev(0, dy),
                )
                for i, (_, dy) in enumerate(ROW)
            ]

    def stage_grad(step, g, finish):
        with jax.named_scope(f"wait_delta_{step}_{g}"):
            arrive(dcp[step, g], f"delta_{step}_{g}")
        with jax.named_scope(f"grad_{step}_{g}"):
            d = dbufs[step, g][...]
            for t in range(ROWS // TILE):
                rows = pl.ds(t * TILE, TILE)
                acc = lax.dot_general(
                    xbufs[step, g][:, rows], d, (((0,), (0,)), ((), ())), preferred_element_type=jnp.float32
                )
                if g > 0:
                    acc = acc + grad[rows]
                if finish is None:
                    grad[rows] = acc
                else:
                    finish(rows, acc * token_scale)

    def finish_first(rows, g):
        w, m, v = adamw(w_now[rows], m_now[rows], v_now[rows], g)
        w_now[rows] = w
        m_now[rows] = m
        v_now[rows] = v

    def finish_last(rows, g):
        grad[rows] = g

    def layer_sum(layer_cps):
        with jax.named_scope("layer_sum"):
            arrive(layer_cps, "layer")
            s = frag[segment(0, 0)].astype(jnp.float32)
            for i in range(len(LAYER)):
                s = s + layer_in[i].astype(jnp.float32)
            partial[...] = s
            cps = []
            for i, dh in enumerate(LAYERS):
                where = pl.ds(pl.multiple_of(lax.rem(zh + dh, 4) * PIECE, 8), PIECE)
                cps.append(remote(partial.at[where], pieces.at[i], ps.at[i], pr.at[i], stack_dev(dh)))
            return cps

    def stack_sum(cps):
        with jax.named_scope("stack_sum"):
            arrive(cps, "stack_sum")
            s = partial[pl.ds(pl.multiple_of(zh * PIECE, 8), PIECE)]
            for i in range(len(LAYERS)):
                s = s + pieces[i]
            mine = pl.ds(pl.multiple_of(layer_index(0, 0) * SEG + zh * PIECE, 8), PIECE)
            total[mine] = s
            out = []
            for i, dh in enumerate(LAYERS):
                out.append(remote(total.at[mine], total.at[mine], qs.at[i], qr.at[i], stack_dev(dh)))
            return out

    def layer_gather(cps):
        with jax.named_scope("layer_gather"):
            arrive(cps, "layer_gather")
            out = []
            for i, (dx, dc) in enumerate(LAYER):
                out.append(
                    remote(
                        total.at[segment(0, 0)], total.at[segment(0, 0)], ts.at[i], tr.at[i], layer_dev(dx, dc)
                    )
                )
            return out

    def outer(cps):
        with jax.named_scope("outer"):
            arrive(cps, "outer")
            get_anchor.wait()
            get_mom.wait()
            a = anchor[...]
            mean = a - total[...] * (1.0 / REPLICAS)
            nm = outer_beta * mom[...] + mean
            newmom[...] = nm
            newanchor[...] = a - outer_rate * (mean + outer_beta * nm)

    held = {}

    def act(kind, step, g):
        if kind == "raw":
            stage_raw(step, g)
        elif kind == "fold":
            stage_fold(step, g)
        elif kind == "delta":
            stage_delta(step, g)
        elif kind == "pass":
            stage_pass(step, g)
        elif kind == "grad":
            final = g == len(GROUPS[step]) - 1
            if final and step == 0:
                get_m.wait()
                get_v.wait()
            stage_grad(step, g, (finish_first, finish_last)[step] if final else None)
        elif kind == "scatter":
            held["sent"] = layer_scatter()
        elif kind == "layer":
            held["sent"] = layer_sum(held["sent"])
        elif kind == "stack":
            held["sent"] = stack_sum(held["sent"])
        elif kind == "gather":
            held["sent"] = layer_gather(held["sent"])
        elif kind == "outer":
            outer(held["sent"])

    open_layers()
    get_cot.wait()
    for k in range(len(UNITS)):
        landed(k)
        before = position
        position += UNITS[k][2]
        for mark, *what in PLAN:
            if before < mark <= position:
                act(*what)
        top_up()
    with jax.named_scope("write"):
        for cp in sends:
            cp.wait_send()


def adamw(w, m, v, g):
    m = beta_first * m + (1.0 - beta_first) * g
    v = beta_second * v + (1.0 - beta_second) * g * g
    w = w.astype(jnp.float32)
    w = w - inner_rate * (m / (jnp.sqrt(v) + adam_eps) + decay_rate * w)
    return w.astype(jnp.bfloat16), m, v


def finish(
    frag_ref, w_ref, m_ref, v_ref, g_ref, mom_ref, anchor_ref,
    merged_out, mom_out, anchor_out, merged, sems, tile_sems,
):
    cps = [
        pltpu.make_async_copy(mom_ref, mom_out, sems.at[0]),
        pltpu.make_async_copy(anchor_ref, anchor_out, sems.at[1]),
    ]
    for cp in cps:
        cp.start()
    first = lax.rem(frag_ref[0], KV) == 0
    lane_first = jnp.where(first, jnp.float32(1.0), jnp.float32(0.0))
    for t in range(ROWS // TILE):
        rows = pl.ds(t * TILE, TILE)
        w, _, _ = adamw(w_ref[rows], m_ref[rows], v_ref[rows], g_ref[rows])
        mixed = anchor_ref[rows]
        for k in range(KV):
            cols = slice(k * HEAD, (k + 1) * HEAD)
            mine = w[:, cols].astype(jnp.float32)
            chosen = lane_first > 0.5 if k == 0 else lane_first < 0.5
            merged[rows, cols] = jnp.where(
                chosen, mix_local * mine + (1.0 - mix_local) * mixed, mine
            ).astype(jnp.bfloat16)
        cp = pltpu.make_async_copy(merged.at[rows], merged_out.at[0, rows], tile_sems.at[t])
        cp.start()
        cps.append(cp)
    for cp in cps:
        cp.wait()


def body(layer_input, cotangent, weight, first_moment, second_moment, key_gain, frag_index, anchor, momentum):
    bf, f32 = jnp.bfloat16, jnp.float32
    dma = pltpu.SemaphoreType.DMA
    any_spec = pl.BlockSpec(memory_space=pltpu.HBM)
    sizes = [GROUPS[s][g] for s, g in EXCH]
    scratch = [pltpu.VMEM((FSDP * n, ROWS), bf) for n in sizes]
    scratch += [pltpu.VMEM((FSDP * n, C), bf) for n in sizes]
    for e, n in zip(EXCH, sizes):
        shape = (3, n, C) if e in STAGED else (3, 2 * n, C) if e in YFIRST else (7, n, C)
        scratch.append(pltpu.VMEM(shape, bf))
    scratch += [pltpu.VMEM((FSDP * n, C), bf) for n in sizes]
    scratch += [pltpu.VMEM((4 * GROUPS[s][g], C), bf) for s, g in STAGED]
    scratch += [pltpu.VMEM((GROUPS[s][g], C), bf) for s, g in YFIRST]
    scratch += [pltpu.VMEM((4 * GROUPS[s][g], C), bf) for s, g in STAGED]
    scratch += [pltpu.VMEM((2 * GROUPS[s][g], C), bf) for s, g in YFIRST]
    scratch += [
        pltpu.VMEM((STEPS, TOK, C), bf),
        pltpu.VMEM((ROWS, HEAD), f32),
        pltpu.VMEM((ROWS, HEAD), f32),
        pltpu.VMEM((ROWS, HEAD), bf),
        pltpu.VMEM((len(LAYER), SEG, HEAD), bf),
        pltpu.VMEM((SEG, HEAD), f32),
        pltpu.VMEM((len(LAYERS), PIECE, HEAD), f32),
        pltpu.VMEM((ROWS, HEAD), f32),
        dma((6,)),
        dma((len(UNITS),)),
        dma((len(UNITS), 7)),
        dma((len(UNITS), 7)),
        dma((len(EXCH), 7)),
        dma((len(EXCH), 7)),
        dma((len(EXCH), 7)),
        dma((len(EXCH), 7)),
        dma((7,)),
        dma((7,)),
        dma((3,)),
        dma((3,)),
        dma((3,)),
        dma((3,)),
        dma((7,)),
        dma((7,)),
        dma((len(EXCH),)),
        dma((len(EXCH),)),
        pltpu.SemaphoreType.REGULAR,
    ]
    vmem_spec = pl.BlockSpec(memory_space=pltpu.VMEM)
    outs = pl.pallas_call(
        kernel,
        name="inner_outer",
        out_shape=(
            pltpu.VMEM((ROWS, C), bf),
            pltpu.VMEM((ROWS, C), f32),
            pltpu.VMEM((ROWS, C), f32),
            pltpu.VMEM((ROWS, C), f32),
            pltpu.VMEM((ROWS, HEAD), f32),
            pltpu.VMEM((ROWS, HEAD), f32),
        ),
        in_specs=[any_spec] * 5 + [vmem_spec, pl.BlockSpec(memory_space=pltpu.SMEM)] + [any_spec] * 2,
        out_specs=(vmem_spec,) * 6,
        scratch_shapes=scratch,
        compiler_params=pltpu.CompilerParams(
            collective_id=0, has_side_effects=True, vmem_limit_bytes=LIMIT
        ),
    )(
        layer_input, cotangent, weight, first_moment, second_moment,
        key_gain.reshape(1, HEAD), frag_index, anchor, momentum,
    )
    outs = [pltpu.with_memory_space_constraint(o, pltpu.VMEM) for o in outs]
    return pl.pallas_call(
        finish,
        name="finish",
        out_shape=[
            jax.ShapeDtypeStruct((1, ROWS, C), bf),
            jax.ShapeDtypeStruct((ROWS, HEAD), f32),
            jax.ShapeDtypeStruct((ROWS, HEAD), f32),
        ],
        in_specs=[pl.BlockSpec(memory_space=pltpu.SMEM)] + [vmem_spec] * 6,
        out_specs=[any_spec] * 3,
        scratch_shapes=[pltpu.VMEM((ROWS, C), bf), dma((2,)), dma((ROWS // TILE,))],
        compiler_params=pltpu.CompilerParams(vmem_limit_bytes=2 << 20),
    )(frag_index, *outs)


def solution(mesh):
    placed = (
        P("replica", None, "fsdp", None),
        P("replica", None, "fsdp", None),
        P("replica", "fsdp", None),
        P("replica", "fsdp", None),
        P("replica", "fsdp", None),
        P(),
        P(),
        P("fsdp", None),
        P("fsdp", None),
    )
    return jax.shard_map(
        body,
        mesh=mesh,
        in_specs=placed,
        out_specs=(P("replica", "fsdp", None), P("fsdp", None), P("fsdp", None)),
        check_vma=False,
    )
```
